256 devices in a mesh: ctx: 32 (over x, z_lo, core), tp: 8 (over y, z_hi).
Axes of the slice: x: 4, y: 4, z: 8 (z_hi: 2, z_lo: 4; z = z_hi * 4 + z_lo), core: 2. Of those that a mesh axis runs over, the one named last changes fastest.
Arguments:
- hyena_feats: bfloat16 [3, 4096, 8192], P(None, 'ctx', 'tp'), may hold values from -6 to 6
- short_taps: float32 [3, 3, 8192], P(None, None, 'tp'), may hold values from -3 to 3
- decay_rate: float32 [16, 8192], P(None, 'tp'), may hold values from 6.1035156e-05 to 0.04
- residue: float32 [16, 8192], P(None, 'tp'), may hold values from -6 to 6
- attn_qkv: bfloat16 [3, 4096, 4096], P(None, 'ctx', 'tp'), may hold values from -7.5 to 7.5
- out_weight: bfloat16 [4096, 8192], P('tp', 'ctx'), may hold values from -0.09375 to 0.09375
Outputs:
- hyena_mixed: bfloat16 [4096, 8192], P('ctx', 'tp')
- attn_mixed: bfloat16 [4096, 8192], P('ctx', 'tp')
The draws below stay inside these ranges and needn't reach their ends.
All inputs are finite; a program needn't handle non-finite values.
Results may differ from the reference program's by a relative error of at most 0.015.
Values may be sent and summed in bfloat16 or wider, within the bound.
No kernel may reach another device: no remote copies, remote signals or barrier semaphores. Data moves between devices by JAX's collectives and lax.ppermute only.
A program may use at most 128 MiB of HBM per device.

```python
import math
import jax
import jax.numpy as jnp
from jax import lax

D = 8192
HEADS = 32
HEAD = 128
ORDER = 16
TAPS = 3
TOKENS = 4096
HH = 4096
N_TP = 8


def draw_attn_qkv(key, part):
    key = jax.random.fold_in(key, 7)
    first_key = jax.random.fold_in(key, 0)
    return jnp.clip(jax.random.normal(first_key, (3, TOKENS, HH), jnp.float32), -6.0, 6.0).astype(jnp.bfloat16)


def levels(own_key, extent, pieces, least, top_value):
    gain = 1.0
    for position, parts in pieces:
        steps = jax.random.uniform(jax.random.fold_in(jax.random.fold_in(own_key, 6), position), (parts,), jnp.float32, least / len(pieces), top_value / len(pieces))
        gain = gain * jnp.repeat(jnp.exp(steps), extent[position] // parts).reshape((-1,) + (1,) * (len(extent) - 1 - position))
    return gain


def centred(own_key, extent, deviation, most, shards=(), dtype=jnp.bfloat16):
    drawn = jax.random.normal(own_key, extent, jnp.float32) * deviation
    if len(shards) > 0:
        drawn = levels(own_key, extent, shards, -0.22, 0.18) * drawn
    return jnp.clip(drawn, min=-most, max=most).astype(dtype)


def setup_inputs(seed: int = 0) -> dict:
    splits = jax.random.split(jax.random.key(seed), 7)
    hyena_feats = centred(splits[0], (3, TOKENS, D), 1.0, 6.0, ((1, 32), (2, 8)))
    short_taps = centred(splits[1], (3, TAPS, D), 0.6, 3.0, ((2, 8),), jnp.float32)
    decay_rate = jnp.clip(jnp.exp(math.log(0.04) - 6.4851847 * jax.random.uniform(splits[2], (ORDER, D), jnp.float32) ** levels(splits[2], (ORDER, D), ((1, 8),), -0.2, 0.2)), 6.103515625e-05, 0.04)
    residue = centred(splits[3], (ORDER, D), 1.0, 6.0, ((1, 8),), jnp.float32)
    attn_qkv = draw_attn_qkv(jax.random.fold_in(splits[6], 71), 0)
    out_weight = centred(splits[5], (HH, D), HH ** -0.5, 0.09375, ((0, 8), (1, 32)))
    return dict(hyena_feats=hyena_feats, short_taps=short_taps, decay_rate=decay_rate, residue=residue, attn_qkv=attn_qkv, out_weight=out_weight)


sub_rows = 16

def featurize(stream_rows, short_taps):
    tap_count = short_taps.shape[1]
    seq_length = stream_rows.shape[1]
    padded = jnp.pad(stream_rows, ((0, 0), (tap_count - 1, 0), (0, 0)))
    summed = jnp.zeros(stream_rows.shape, jnp.float32)
    for tap_index in range(tap_count):
        lo_edge = tap_count - 1 - tap_index
        summed = summed + short_taps[:, tap_index, None, :] * padded[:, lo_edge:lo_edge + seq_length, :]
    return summed

def filter_tables(decay_rate, residue):
    order_count = decay_rate.shape[0]
    offsets = jnp.arange(sub_rows).astype(jnp.float32)
    weight = residue * jnp.sqrt(-jnp.expm1(-2.0 * decay_rate) / order_count)
    kernel = lax.optimization_barrier(jnp.sum(weight[None] * jnp.exp(-decay_rate[None] * offsets[:, None, None]), axis=1))
    later = jnp.arange(sub_rows)[:, None]
    earlier = jnp.arange(sub_rows)[None, :]
    lagged = kernel[jnp.maximum(later - earlier, 0)]
    toeplitz = jnp.where((later >= earlier)[:, :, None], lagged, 0.0)
    end_table = jnp.exp(-decay_rate[None] * (sub_rows - 1.0 - offsets)[:, None, None])
    out_table = weight[None] * jnp.exp(-decay_rate[None] * (offsets + 1.0)[:, None, None])
    return (toeplitz, end_table, out_table)

def block_terms(product, toeplitz, end_table):
    chans = product.shape[-1]
    sub_blocks = product.reshape(-1, sub_rows, chans)
    inside = jnp.einsum('tsc,nsc->ntc', toeplitz, sub_blocks, precision=lax.Precision.HIGHEST)
    local_ends = jnp.einsum('src,nsc->nrc', end_table, sub_blocks, precision=lax.Precision.HIGHEST)
    return (inside, local_ends)

def carry_states(local_ends, step_decay):

    def advance(running_state, block_ends):
        return (step_decay * running_state + block_ends, running_state)
    final_state, states_before = lax.scan(advance, jnp.zeros(step_decay.shape, jnp.float32), local_ends)
    return (states_before, final_state)

def finish_conv(inside, states_before, out_table):
    carried = jnp.einsum('trc,nrc->ntc', out_table, states_before, precision=lax.Precision.HIGHEST)
    return (inside + carried).reshape(-1, inside.shape[-1])

def reference(hyena_feats, short_taps, decay_rate, residue, attn_qkv, out_weight):
    featured = featurize(hyena_feats.astype(jnp.float32), short_taps)
    product = featured[1] * featured[2]
    toeplitz, end_table, out_table = filter_tables(decay_rate, residue)
    inside, local_ends = block_terms(product, toeplitz, end_table)
    step_decay = jnp.exp(-decay_rate * sub_rows)
    states_before, final_state = carry_states(local_ends, step_decay)
    conv = finish_conv(inside, states_before, out_table)
    hyena_mixed = (featured[0] * conv).astype(jnp.bfloat16)
    block_rows = 256 if TOKENS % 256 == 0 else TOKENS
    block_count = TOKENS // block_rows
    scale = 1.0 / math.sqrt(HEAD)
    queries = attn_qkv[0].astype(jnp.float32).reshape(block_count, block_rows, HEADS, HEAD)
    key_rows = attn_qkv[1].astype(jnp.float32).reshape(TOKENS, HEADS, HEAD)
    value_rows = attn_qkv[2].astype(jnp.float32).reshape(TOKENS, HEADS, HEAD)
    key_positions = jnp.arange(TOKENS).astype(jnp.int32)

    def one_block(inputs):
        query_block, block_index = inputs
        scores = jnp.einsum('rhd,khd->hrk', query_block, key_rows, precision=lax.Precision.HIGHEST) * scale
        query_positions = (block_index * block_rows + jnp.arange(block_rows)).astype(jnp.int32)
        visible = key_positions[None, None, :] <= query_positions[None, :, None]
        row_max = lax.optimization_barrier(jnp.max(jnp.where(visible, scores, -jnp.inf), axis=-1))
        expo = jnp.where(visible, jnp.exp(scores - row_max[..., None]), 0.0)
        totals = lax.optimization_barrier(jnp.sum(expo, axis=-1))
        weights = lax.optimization_barrier(expo.astype(jnp.bfloat16)).astype(jnp.float32)
        output = jnp.einsum('hrk,khd->rhd', weights, value_rows, precision=lax.Precision.HIGHEST)
        output = output / totals.T[:, :, None]
        return output.astype(jnp.bfloat16).reshape(block_rows, HEADS * HEAD)
    attended = lax.map(one_block, (queries, jnp.arange(block_count).astype(jnp.int32)))
    attended = attended.reshape(TOKENS, HEADS * HEAD)
    group_width = HEADS * HEAD // N_TP
    summed = jnp.zeros((TOKENS, D), jnp.float32)
    for group_index in range(N_TP):
        lo_col = group_index * group_width
        partial_value = jnp.dot(attended[:, lo_col:lo_col + group_width], out_weight[lo_col:lo_col + group_width], preferred_element_type=jnp.float32)
        summed = summed + lax.optimization_barrier(partial_value.astype(jnp.bfloat16)).astype(jnp.float32)
    attn_mixed = summed.astype(jnp.bfloat16)
    return (hyena_mixed, attn_mixed)
```

```python
import math

import jax
import jax.numpy as jnp
from jax import lax
from jax.experimental import pallas as pl
from jax.experimental.pallas import tpu as pltpu
from jax.sharding import Mesh, PartitionSpec as P

HEAD = 128
NX, NZ1, NZ0, NK, NY, NH = 4, 2, 2, 2, 4, 2
NZ = NZ1 * NZ0
ALL = ("x", "z1", "z0", "k", "y", "h")
SIZES = dict(x=NX, z1=NZ1, z0=NZ0, k=NK, y=NY, h=NH)
SCALE = math.log2(math.e) / math.sqrt(HEAD)
VMEM = 48 * 1024 * 1024


def linear(**c):
    index = 0
    for name in ALL:
        index = index * SIZES[name] + c[name]
    return index


def places():
    for index in range(256):
        rest, c = index, {}
        for name in reversed(ALL):
            c[name] = rest % SIZES[name]
            rest //= SIZES[name]
        yield c


def moved(change):
    pairs = []
    for c in places():
        d = change(**c)
        if d is not None:
            pairs.append((linear(**c), linear(**dict(c, **d))))
    return pairs


def next_ctx(x, z1, z0, k, **_):
    place = ((x * NZ1 + z1) * NZ0 + z0) * NK + k + 1
    if place == NX * NZ * NK:
        return None
    return dict(x=place // (NZ * NK), z1=place // 4 % 2, z0=place // 2 % 2, k=place % 2)


def along_z(steps):
    def change(z1, z0, **_):
        z = (2 * z1 + z0 + steps) % NZ
        return dict(z1=z // 2, z0=z % 2)

    return moved(change)


def place_weight(x, z1, z0, k, y, h):
    return dict(x=(x + y) % NX, z1=h, z0=z0, k=k, y=x, h=z1)


SMEM = pl.BlockSpec(memory_space=pltpu.SMEM)
FAST = pl.BlockSpec(memory_space=pltpu.VMEM)
SLOW = pl.BlockSpec(memory_space=pltpu.HBM)
ANY = pl.BlockSpec(memory_space=pl.ANY)


def local_call(kernel, out_shape, specs, name, flops, scratch=(), after=()):
    count = len(specs)

    def body(*refs):
        kernel(*refs[:count], *refs[count + len(after) :])

    call = pl.pallas_call(
        body,
        out_shape=out_shape,
        in_specs=list(specs) + [ANY] * len(after),
        out_specs=jax.tree.map(lambda _: FAST, out_shape),
        scratch_shapes=list(scratch),
        compiler_params=pltpu.CompilerParams(vmem_limit_bytes=VMEM),
        cost_estimate=pl.CostEstimate(flops=flops, bytes_accessed=2_000_000, transcendentals=0),
        name=name,
    )

    def placed(operand, spec):
        return pltpu.with_memory_space_constraint(operand, pltpu.HBM) if spec is SLOW else operand

    return lambda *operands: call(*map(placed, operands, specs), *after)


def gate(value, *after):
    return pl.pallas_call(
        lambda *refs: None,
        out_shape=jax.ShapeDtypeStruct(value.shape, value.dtype),
        in_specs=[ANY] * (1 + len(after)),
        out_specs=ANY,
        input_output_aliases={0: 0},
        name="gate",
    )(value, *after)


def started(sems, pairs):
    copies = [pltpu.make_async_copy(a, b, sems.at[i]) for i, (a, b) in enumerate(pairs)]
    for copy in copies:
        copy.start()
    return copies


def finished(copies):
    for copy in copies:
        copy.wait()


def fill_ext(x, halo_ref, ext, streams):
    for slot, stream in enumerate(streams):
        ext[slot, 6:8] = halo_ref[stream]
        for lo in range(0, x.shape[1], 32):
            ext[slot, lo + 8 : lo + 40] = x[slot, lo : lo + 32].astype(jnp.float32)


def featured_rows(ext, taps_ref, slot, stream, lo, rows):
    taps = taps_ref[stream]
    total = taps[0:1] * ext[slot, lo + 8 : lo + 8 + rows]
    for j in (1, 2):
        total += taps[j : j + 1] * ext[slot, lo + 8 - j : lo + 8 - j + rows]
    return total


def ends_kernel(
    feats, halo_ref, taps_hbm, decay_hbm, out_ref, prod, gate_rows, rate, x, taps, ext, sems
):
    finished(started(sems, ((feats, x), (taps_hbm, taps), (decay_hbm, rate))))
    rows, order = x.shape[1], rate.shape[0]
    fill_ext(x, halo_ref, ext, (0, 1, 2))
    for lo in range(0, rows, 16):
        gate_rows[lo : lo + 16] = featured_rows(ext, taps, 0, 0, lo, 16)
        first = featured_rows(ext, taps, 1, 1, lo, 16)
        prod[lo : lo + 16] = first * featured_rows(ext, taps, 2, 2, lo, 16)
    decay = jnp.exp(-rate[...])

    def body(i, state):
        block = prod[pl.ds(pl.multiple_of(i * 8, 8), 8), :]
        for j in range(8):
            state = decay * state + block[j : j + 1]
        return state

    state = lax.fori_loop(0, rows // 8, body, jnp.zeros(rate.shape, jnp.float32))
    for j in range(state.shape[1] // HEAD):
        block = state[:, j * HEAD : (j + 1) * HEAD]
        high = block.astype(jnp.bfloat16)
        out_ref[0, j * order : (j + 1) * order] = high
        out_ref[1, j * order : (j + 1) * order] = (block - high.astype(jnp.float32)).astype(
            jnp.bfloat16
        )


def combine_kernel(place_ref, decay_ref, own_ref, other_ref, out_ref, ends):
    x, z, k = place_ref[0], place_ref[1], place_ref[2]
    rate = decay_ref[...]
    order = rate.shape[0]

    def over(blocks):
        return jnp.exp(rate * (-128.0 * jnp.maximum(blocks, 0).astype(jnp.float32)))

    for row in range(NX):
        for side, ref in enumerate((own_ref, other_ref)):
            both = ref[row, 2 * NZ].astype(jnp.float32) + ref[row, 2 * NZ + 1].astype(jnp.float32)
            for j in range(rate.shape[1] // HEAD):
                lanes = slice(j * HEAD, (j + 1) * HEAD)
                ends[row, side, :, lanes] = both[j * order : (j + 1) * order]

    def end_of(row, core):
        return ends[row, jnp.where(k == core, 0, 1)]

    step, across, rest = over(jnp.int32(1)), over(jnp.int32(NZ * NK)), over(NZ * NK - NK * z - NK)
    earlier = jnp.zeros(rate.shape, jnp.float32)
    for row in range(NX - 1):
        whole = rest * (step * end_of(row, 0) + end_of(row, 1))
        earlier = jnp.where(x > row, across * earlier + whole, earlier)
    for target in range(NZ):
        total = over(NK * target + k) * earlier
        for core in range(NK):
            blocks = (NK * target + k) - (NK * z + core) - 1
            total = total + jnp.where(blocks >= 0, over(blocks) * end_of(x, core), 0.0)
        out_ref[target] = total


def mix_kernel(decay_ref, rho_ref, parts_ref, prod, gate_rows, out_ref):
    rows, width = prod.shape
    decay = jnp.exp(-decay_ref[...])
    start = parts_ref[0]
    for z in range(1, NZ):
        start = start + parts_ref[z]
    rho = rho_ref[...]
    sub = lax.broadcasted_iota(jnp.int32, (8, width), 0)

    def body(i, state):
        base = pl.multiple_of(i * 16, 16)
        mixed = []
        for half in range(2):
            block = prod[pl.ds(base + 8 * half, 8), :]
            conv = jnp.zeros((8, width), jnp.float32)
            for j in range(8):
                state = decay * state + block[j : j + 1]
                row = jnp.sum(rho * state, axis=0, keepdims=True)
                conv = jnp.where(sub == j, row, conv)
            mixed.append(conv * gate_rows[pl.ds(base + 8 * half, 8), :])
        out_ref[pl.ds(base, 16), :] = jnp.concatenate(mixed, axis=0).astype(jnp.bfloat16)
        return state

    lax.fori_loop(0, rows // 16, body, start)


def pack_kernel(qkv, feats, out_ref, halo_ref, tail, sems):
    rows = qkv.shape[1]
    pairs = [(feats.at[:, pl.ds(rows - 16, 16), :], tail)]
    for head in range(NZ):
        lanes = pl.ds(head * HEAD, HEAD)
        pairs += [(qkv.at[i, :, lanes], out_ref.at[head, i]) for i in range(3)]
    finished(started(sems, pairs))
    halo_ref[...] = tail[:, 14:16].astype(jnp.float32)


def halves_kernel(place_ref, weight_ref, same_ref, other_ref):
    for half in range(NZ0):

        @pl.when(place_ref[0] % NZ0 == half)
        def _():
            for ref, z0 in ((same_ref, half), (other_ref, 1 - half)):
                for part in range(NZ1):
                    lo = (2 * part + z0) * HEAD
                    ref[part] = weight_ref[lo : lo + HEAD]


def stack_kernel(place_ref, *refs):
    for steps, ref in enumerate(refs[:-1]):
        refs[-1][(place_ref[0] + NZ - steps) % NZ] = ref[...]


def spread_kernel(qkv_ref, ends_ref, kv_ref, out_ref):
    for z in range(NZ):
        kv_ref[z] = qkv_ref[z, 1:]
        for i in range(out_ref.shape[0]):
            out_ref[i, 2 * z : 2 * z + 2] = qkv_ref[z, 1:]
    for i in range(out_ref.shape[0]):
        out_ref[i, 2 * NZ :] = ends_ref[...]


def folded(q, sets, top, total, acc, visible=None):
    keys = jnp.concatenate([a[:, 0].reshape(-1, HEAD) for a in sets], axis=0)
    values = jnp.concatenate([a[:, 1].reshape(-1, HEAD) for a in sets], axis=0)
    s = lax.dot_general(keys, q, (((1,), (1,)), ((), ())), preferred_element_type=jnp.float32)
    if visible is not None:
        s = jnp.where(visible, s, -1e30)
    new = jnp.maximum(top, jnp.max(s, axis=0, keepdims=True))
    p = jnp.exp2((s - new) * SCALE)
    again = jnp.exp2((top - new) * SCALE)
    added = jnp.dot(values.T, p.astype(jnp.bfloat16), preferred_element_type=jnp.float32)
    return new, total * again + jnp.sum(p, axis=0, keepdims=True), acc * again + added


def near_kernel(place_ref, qkv_ref, a, b, top_ref, total_ref, acc_ref):
    k = place_ref[1]
    rows = NZ * HEAD
    col = lax.broadcasted_iota(jnp.int32, (1, rows), 1)
    row = lax.broadcasted_iota(jnp.int32, (2 * rows, 1), 0)
    core = jnp.where(row < rows, k, 1 - k)
    here = (2 * (col // HEAD) + k) * HEAD + col % HEAD
    there = (2 * ((row % rows) // HEAD) + core) * HEAD + row % HEAD
    lowest = jnp.full((1, rows), -1e30, jnp.float32)
    top_ref[...], total_ref[...], acc_ref[...] = folded(
        qkv_ref[:, 0].reshape(rows, HEAD),
        (a[...], b[...]),
        lowest,
        jnp.zeros((1, rows), jnp.float32),
        jnp.zeros((HEAD, rows), jnp.float32),
        there <= here,
    )


def pairs_of(ref, row):
    return ref[row, 0 : 2 * NZ].reshape(NZ, 2, HEAD, HEAD)


def far_kernel(
    place_ref, qkv_ref, top_ref, total_ref, acc_ref, a_ref, b_ref, out_ref, top, total, acc
):
    q = qkv_ref[:, 0].reshape(NZ * HEAD, HEAD)
    top[...], total[...], acc[...] = top_ref[...], total_ref[...], acc_ref[...]
    for row in range(NX - 1):

        @pl.when(place_ref[0] > row)
        def _():
            top[...], total[...], acc[...] = folded(
                q, (pairs_of(a_ref, row), pairs_of(b_ref, row)), top[...], total[...], acc[...]
            )

    result = (acc[...] / total[...]).T.astype(jnp.bfloat16).reshape(out_ref.shape[1:])
    for h in range(NH):
        out_ref[h] = result


def project_kernel(place_ref, g0, g1, g2, g3, w_hbm, mine_ref, other_ref, held, parts, acc, sems):
    y, z0 = place_ref[0], place_ref[1]
    copies = started(sems, [(w_hbm.at[i], parts.at[i]) for i in range(NX)])
    for step, group in zip((0, 1, 3, 2), (g0, g1, g2, g3)):
        held[step] = group[...]
    for i in range(NX):
        step = (2 * y - i + NX) % NX
        heads = jnp.concatenate([held[step, j] for j in range(NH * NZ1)], axis=1)
        copies[i].wait()
        for k in range(NK):
            for b in range(2):
                columns = [parts[i, k, 2 * h + b].reshape(2 * HEAD, 256) for h in range(NH)]
                term = jnp.dot(
                    heads, jnp.concatenate(columns, axis=0), preferred_element_type=jnp.float32
                )
                lanes = slice(b * 256, b * 256 + 256)
                if i == 0:
                    acc[k, :, lanes] = term
                else:
                    acc[k, :, lanes] += term
    rows = mine_ref.shape[0]
    near_rows = pl.ds(pl.multiple_of(z0 * rows, rows), rows)
    far_rows = pl.ds(pl.multiple_of((1 - z0) * rows, rows), rows)
    for b in range(2):
        for k in range(NK):
            lo = (2 * b + k) * 256
            lanes = slice(b * 256, b * 256 + 256)
            mine_ref[:, lo : lo + 256] = acc[k, near_rows, lanes]
            other_ref[:, lo : lo + 256] = acc[k, far_rows, lanes].astype(jnp.bfloat16)


def per_device(hyena_feats, short_taps, decay_rate, residue, attn_qkv, out_weight):
    rows, width = hyena_feats.shape[1:]
    x, k, y = lax.axis_index("x"), lax.axis_index("k"), lax.axis_index("y")
    z1, z0 = lax.axis_index("z1"), lax.axis_index("z0")
    swap = [(0, 1), (1, 0)]
    short = jax.ShapeDtypeStruct
    bf16, f32 = jnp.bfloat16, jnp.float32
    dma = pltpu.SemaphoreType.DMA

    packed, tail = local_call(
        pack_kernel,
        (short((NZ, 3, rows, HEAD), bf16), short((3, 2, width), f32)),
        (SLOW, SLOW),
        "pack",
        10**8,
        (pltpu.VMEM((3, 16, width), bf16), dma((1 + 3 * NZ,))),
    )(attn_qkv, hyena_feats)
    qkv = lax.all_to_all(packed, ("z1", "z0"), 0, 0)
    halo = lax.ppermute(tail, ALL, moved(next_ctx))
    plane = short((rows, width), f32)
    poles = short(decay_rate.shape, f32)
    ends, prod, gate_rows, rate = local_call(
        ends_kernel,
        (short((2, rows, HEAD), bf16), plane, plane, poles),
        (SLOW, FAST, SLOW, SLOW),
        "ends",
        10**9,
        (
            pltpu.VMEM((3, rows, width), bf16),
            pltpu.VMEM(short_taps.shape, f32),
            pltpu.VMEM((3, rows + 8, width), f32),
            dma((3,)),
        ),
    )(hyena_feats, halo, short_taps, decay_rate)
    moved_weight = lax.ppermute(out_weight, ALL, moved(place_weight))
    kv, spread = local_call(
        spread_kernel,
        (short((NZ, 2, rows, HEAD), bf16), short((NX, 2 * NZ + 2, rows, HEAD), bf16)),
        (FAST, FAST),
        "spread",
        10**8,
        after=(moved_weight,),
    )(qkv, ends)
    near = lax.ppermute(kv, "k", swap)
    far_own = lax.all_to_all(spread, "x", 0, 0)
    far_other = lax.ppermute(far_own, "k", swap)

    z = (2 * z1 + z0).reshape(1)
    half = short((NZ1, HEAD, out_weight.shape[1]), bf16)
    same, opposite = local_call(
        halves_kernel, (half, half), (SMEM, FAST), "halves", 10**8, after=(spread,)
    )(z, moved_weight)
    arrived = [same] + [
        lax.ppermute(opposite if steps % 2 else same, ALL, along_z(steps)) for steps in (1, 2, 3)
    ]
    placed = local_call(
        stack_kernel, short((NZ, *half.shape), bf16), (SMEM,) + (FAST,) * NZ, "stack", 10**8,
        after=(far_own,),
    )(z, *arrived)
    weight = lax.all_gather(placed, ("x", "k")).reshape(NX, NK, *placed.shape)

    where = jnp.stack([x, k])
    line = short((1, NZ * rows), f32)
    square = short((HEAD, NZ * rows), f32)
    partial = local_call(
        near_kernel, (line, line, square), (SMEM, FAST, FAST, FAST), "near", 2 * 10**9
    )(where, qkv, kv, near)
    attended = local_call(
        far_kernel,
        short((NH, NZ1, NZ0 * rows, HEAD), bf16),
        (SMEM,) + (FAST,) * 6,
        "far",
        4 * 10**9,
        [pltpu.VMEM(part.shape, f32) for part in (line, line, square)],
    )(where, qkv, *partial, far_own, far_other)
    group = lax.all_to_all(attended.reshape(NH * NZ1, NZ0 * rows, HEAD), ("h", "z1"), 0, 0)
    groups = [group] + [
        lax.ppermute(group, "y", [(i, (i + step) % NY) for i in range(NY)]) for step in (1, 3, 2)
    ]

    parts = local_call(
        combine_kernel,
        short((NZ, *poles.shape), f32),
        (SMEM, FAST, FAST, FAST),
        "combine",
        10**8,
        (pltpu.VMEM((NX, NK, *poles.shape), f32),),
        after=(group,),
    )(jnp.stack([x, 2 * z1 + z0, k]), rate, far_own, far_other)
    parts = lax.all_to_all(parts, ("z1", "z0"), 0, 0)

    mine, other = local_call(
        project_kernel,
        (short((rows, width), f32), short((rows, width), bf16)),
        (SMEM,) + (FAST,) * 4 + (SLOW,),
        "project",
        2 * 10**9,
        (
            pltpu.VMEM((NY, *group.shape), bf16),
            pltpu.VMEM(weight.shape, bf16),
            pltpu.VMEM((NK, NZ0 * rows, width // 2), f32),
            dma((NX,)),
        ),
    )(jnp.stack([y, z0]), *groups, weight)
    received = lax.ppermute(other, "z0", swap)

    rho = residue * jnp.sqrt(-jnp.expm1(-2.0 * rate) / rate.shape[0])
    hyena_mixed = local_call(
        mix_kernel,
        short((rows, width), bf16),
        (FAST,) * 5,
        "mix",
        4 * 10**9,
    )(rate, rho, parts, prod, gate_rows)
    return hyena_mixed, (mine + received.astype(f32)).astype(bf16)


def solution(mesh):
    fine = Mesh(mesh.devices.reshape(NX, NZ1, NZ0, NK, NY, NH), ALL)
    ctx, tp = ("x", "z1", "z0", "k"), ("y", "h")
    return jax.shard_map(
        per_device,
        mesh=fine,
        in_specs=(
            P(None, ctx, tp),
            P(None, None, tp),
            P(None, tp),
            P(None, tp),
            P(None, ctx, tp),
            P(tp, ctx),
        ),
        out_specs=(P(ctx, tp), P(ctx, tp)),
        check_vma=False,
    )
```

```python
import math

import jax
import jax.numpy as jnp
from jax import lax
from jax.experimental import pallas as pl
from jax.experimental.pallas import tpu as pltpu
from jax.sharding import Mesh, PartitionSpec as P

HEAD = 128
NX, NZ1, NZ0, NK, NY, NH = 4, 2, 2, 2, 4, 2
NZ = NZ1 * NZ0
ALL = ("x", "z1", "z0", "k", "y", "h")
SIZES = dict(x=NX, z1=NZ1, z0=NZ0, k=NK, y=NY, h=NH)
SCALE = math.log2(math.e) / math.sqrt(HEAD)
VMEM = 48 * 1024 * 1024


def linear(**c):
    index = 0
    for name in ALL:
        index = index * SIZES[name] + c[name]
    return index


def places():
    for index in range(256):
        rest, c = index, {}
        for name in reversed(ALL):
            c[name] = rest % SIZES[name]
            rest //= SIZES[name]
        yield c


def moved(change):
    pairs = []
    for c in places():
        d = change(**c)
        if d is not None:
            pairs.append((linear(**c), linear(**dict(c, **d))))
    return pairs


def next_ctx(x, z1, z0, k, **_):
    place = ((x * NZ1 + z1) * NZ0 + z0) * NK + k + 1
    if place == NX * NZ * NK:
        return None
    return dict(x=place // (NZ * NK), z1=place // 4 % 2, z0=place // 2 % 2, k=place % 2)


def along_z(steps):
    def change(z1, z0, **_):
        z = (2 * z1 + z0 + steps) % NZ
        return dict(z1=z // 2, z0=z % 2)

    return moved(change)


def place_weight(x, z1, z0, k, y, h):
    return dict(x=(x + y) % NX, z1=h, z0=z0, k=k, y=x, h=z1)


SMEM = pl.BlockSpec(memory_space=pltpu.SMEM)
FAST = pl.BlockSpec(memory_space=pltpu.VMEM)
SLOW = pl.BlockSpec(memory_space=pltpu.HBM)
ANY = pl.BlockSpec(memory_space=pl.ANY)


def local_call(kernel, out_shape, specs, name, flops, scratch=(), after=()):
    count = len(specs)

    def body(*refs):
        kernel(*refs[:count], *refs[count + len(after) :])

    call = pl.pallas_call(
        body,
        out_shape=out_shape,
        in_specs=list(specs) + [ANY] * len(after),
        out_specs=jax.tree.map(lambda _: FAST, out_shape),
        scratch_shapes=list(scratch),
        compiler_params=pltpu.CompilerParams(vmem_limit_bytes=VMEM),
        cost_estimate=pl.CostEstimate(flops=flops, bytes_accessed=2_000_000, transcendentals=0),
        name=name,
    )

    def placed(operand, spec):
        return pltpu.with_memory_space_constraint(operand, pltpu.HBM) if spec is SLOW else operand

    return lambda *operands: call(*map(placed, operands, specs), *after)


def gate(value, *after):
    return pl.pallas_call(
        lambda *refs: None,
        out_shape=jax.ShapeDtypeStruct(value.shape, value.dtype),
        in_specs=[ANY] * (1 + len(after)),
        out_specs=ANY,
        input_output_aliases={0: 0},
        name="gate",
    )(value, *after)


def started(sems, pairs):
    copies = [pltpu.make_async_copy(a, b, sems.at[i]) for i, (a, b) in enumerate(pairs)]
    for copy in copies:
        copy.start()
    return copies


def finished(copies):
    for copy in copies:
        copy.wait()


def fill_ext(x, halo_ref, ext, streams):
    for slot, stream in enumerate(streams):
        ext[slot, 6:8] = halo_ref[stream]
        for lo in range(0, x.shape[1], 32):
            ext[slot, lo + 8 : lo + 40] = x[slot, lo : lo + 32].astype(jnp.float32)


def featured_rows(ext, taps_ref, slot, stream, lo, rows):
    taps = taps_ref[stream]
    total = taps[0:1] * ext[slot, lo + 8 : lo + 8 + rows]
    for j in (1, 2):
        total += taps[j : j + 1] * ext[slot, lo + 8 - j : lo + 8 - j + rows]
    return total


def ends_kernel(
    feats, halo_ref, taps_hbm, decay_hbm, out_ref, prod, gate_rows, rate, x, taps, ext, sems
):
    finished(started(sems, ((feats, x), (taps_hbm, taps), (decay_hbm, rate))))
    rows, order = x.shape[1], rate.shape[0]
    fill_ext(x, halo_ref, ext, (0, 1, 2))
    for lo in range(0, rows, 16):
        gate_rows[lo : lo + 16] = featured_rows(ext, taps, 0, 0, lo, 16)
        first = featured_rows(ext, taps, 1, 1, lo, 16)
        prod[lo : lo + 16] = first * featured_rows(ext, taps, 2, 2, lo, 16)
    decay = jnp.exp(-rate[...])

    def body(i, state):
        block = prod[pl.ds(pl.multiple_of(i * 8, 8), 8), :]
        for j in range(8):
            state = decay * state + block[j : j + 1]
        return state

    state = lax.fori_loop(0, rows // 8, body, jnp.zeros(rate.shape, jnp.float32))
    for j in range(state.shape[1] // HEAD):
        block = state[:, j * HEAD : (j + 1) * HEAD]
        high = block.astype(jnp.bfloat16)
        out_ref[0, j * order : (j + 1) * order] = high
        out_ref[1, j * order : (j + 1) * order] = (block - high.astype(jnp.float32)).astype(
            jnp.bfloat16
        )


def combine_kernel(place_ref, decay_ref, own_ref, other_ref, out_ref, ends):
    x, z, k = place_ref[0], place_ref[1], place_ref[2]
    rate = decay_ref[...]
    order = rate.shape[0]

    def over(blocks):
        return jnp.exp(rate * (-128.0 * jnp.maximum(blocks, 0).astype(jnp.float32)))

    for row in range(NX):
        for side, ref in enumerate((own_ref, other_ref)):
            both = ref[row, 2 * NZ].astype(jnp.float32) + ref[row, 2 * NZ + 1].astype(jnp.float32)
            for j in range(rate.shape[1] // HEAD):
                lanes = slice(j * HEAD, (j + 1) * HEAD)
                ends[row, side, :, lanes] = both[j * order : (j + 1) * order]

    def end_of(row, core):
        return ends[row, jnp.where(k == core, 0, 1)]

    step, across, rest = over(jnp.int32(1)), over(jnp.int32(NZ * NK)), over(NZ * NK - NK * z - NK)
    earlier = jnp.zeros(rate.shape, jnp.float32)
    for row in range(NX - 1):
        whole = rest * (step * end_of(row, 0) + end_of(row, 1))
        earlier = jnp.where(x > row, across * earlier + whole, earlier)
    for target in range(NZ):
        total = over(NK * target + k) * earlier
        for core in range(NK):
            blocks = (NK * target + k) - (NK * z + core) - 1
            total = total + jnp.where(blocks >= 0, over(blocks) * end_of(x, core), 0.0)
        out_ref[target] = total


def mix_kernel(decay_ref, rho_ref, parts_ref, prod, gate_rows, out_ref):
    rows, width = prod.shape
    decay = jnp.exp(-decay_ref[...])
    start = parts_ref[0]
    for z in range(1, NZ):
        start = start + parts_ref[z]
    rho = rho_ref[...]
    sub = lax.broadcasted_iota(jnp.int32, (8, width), 0)

    def body(i, state):
        base = pl.multiple_of(i * 16, 16)
        mixed = []
        for half in range(2):
            block = prod[pl.ds(base + 8 * half, 8), :]
            conv = jnp.zeros((8, width), jnp.float32)
            for j in range(8):
                state = decay * state + block[j : j + 1]
                row = jnp.sum(rho * state, axis=0, keepdims=True)
                conv = jnp.where(sub == j, row, conv)
            mixed.append(conv * gate_rows[pl.ds(base + 8 * half, 8), :])
        out_ref[pl.ds(base, 16), :] = jnp.concatenate(mixed, axis=0).astype(jnp.bfloat16)
        return state

    lax.fori_loop(0, rows // 16, body, start)


def tail_kernel(feats, halo_ref, tail, sems):
    rows = feats.shape[1]
    finished(started(sems, [(feats.at[:, pl.ds(rows - 16, 16), :], tail)]))
    halo_ref[...] = tail[:, 14:16].astype(jnp.float32)


def pack_kernel(qkv, out_ref, sems):
    pairs = []
    for head in range(NZ):
        lanes = pl.ds(head * HEAD, HEAD)
        pairs += [(qkv.at[i, :, lanes], out_ref.at[head, i]) for i in range(3)]
    finished(started(sems, pairs))


def halves_kernel(place_ref, weight_ref, same_ref, other_ref):
    for half in range(NZ0):

        @pl.when(place_ref[0] % NZ0 == half)
        def _():
            for ref, z0 in ((same_ref, half), (other_ref, 1 - half)):
                for part in range(NZ1):
                    lo = (2 * part + z0) * HEAD
                    ref[part] = weight_ref[lo : lo + HEAD]


def stack_kernel(place_ref, *refs):
    for steps, ref in enumerate(refs[:-1]):
        refs[-1][(place_ref[0] + NZ - steps) % NZ] = ref[...]


def spread_kernel(qkv_ref, ends_ref, out_ref):
    for z in range(NZ):
        for i in range(out_ref.shape[0]):
            out_ref[i, 2 * z : 2 * z + 2] = qkv_ref[z, 1:]
    for i in range(out_ref.shape[0]):
        out_ref[i, 2 * NZ :] = ends_ref[...]


def folded(q, pairs, top, total, acc, visible=None):
    keys = pairs[:, 0].reshape(-1, HEAD)
    values = pairs[:, 1].reshape(-1, HEAD)
    s = lax.dot_general(keys, q, (((1,), (1,)), ((), ())), preferred_element_type=jnp.float32)
    if visible is not None:
        s = jnp.where(visible, s, -1e30)
    new = jnp.maximum(top, jnp.max(s, axis=0, keepdims=True))
    p = jnp.exp2((s - new) * SCALE)
    again = jnp.exp2((top - new) * SCALE)
    added = jnp.dot(values.T, p.astype(jnp.bfloat16), preferred_element_type=jnp.float32)
    return new, total * again + jnp.sum(p, axis=0, keepdims=True), acc * again + added


def pairs_of(ref, row):
    return ref[row, 0 : 2 * NZ].reshape(NZ, 2, HEAD, HEAD)


def fold_rows(x, q, ref, top, total, acc):
    for row in range(NX - 1):

        @pl.when(x > row)
        def _():
            top[...], total[...], acc[...] = folded(
                q, pairs_of(ref, row), top[...], total[...], acc[...]
            )


def own_kernel(place_ref, qkv_ref, kv_ref, top_ref, total_ref, acc_ref):
    x = place_ref[0]
    rows = NZ * HEAD
    q = qkv_ref[:, 0].reshape(rows, HEAD)
    col = lax.broadcasted_iota(jnp.int32, (1, rows), 1)
    row = lax.broadcasted_iota(jnp.int32, (rows, 1), 0)
    lowest = jnp.full((1, rows), -1e30, jnp.float32)
    nothing = jnp.zeros((1, rows), jnp.float32), jnp.zeros((HEAD, rows), jnp.float32)
    top_ref[...], total_ref[...], acc_ref[...] = folded(
        q, pairs_of(kv_ref, x), lowest, *nothing, row <= col
    )
    fold_rows(x, q, kv_ref, top_ref, total_ref, acc_ref)


def other_kernel(
    place_ref, qkv_ref, top_ref, total_ref, acc_ref, kv_ref, out_ref, top, total, acc
):
    x, k = place_ref[0], place_ref[1]
    rows = NZ * HEAD
    q = qkv_ref[:, 0].reshape(rows, HEAD)
    col = lax.broadcasted_iota(jnp.int32, (1, rows), 1)
    row = lax.broadcasted_iota(jnp.int32, (rows, 1), 0)
    here = (2 * (col // HEAD) + k) * HEAD + col % HEAD
    there = (2 * (row // HEAD) + 1 - k) * HEAD + row % HEAD
    top[...], total[...], acc[...] = folded(
        q, pairs_of(kv_ref, x), top_ref[...], total_ref[...], acc_ref[...], there <= here
    )
    fold_rows(x, q, kv_ref, top, total, acc)
    result = (acc[...] / total[...]).T.astype(jnp.bfloat16).reshape(out_ref.shape[1:])
    for h in range(NH):
        out_ref[h] = result


def project_kernel(place_ref, g0, g1, g2, g3, w_hbm, mine_ref, other_ref, held, parts, acc, sems):
    y, z0 = place_ref[0], place_ref[1]
    copies = started(sems, [(w_hbm.at[i], parts.at[i]) for i in range(NX)])
    for step, group in zip((0, 1, 3, 2), (g0, g1, g2, g3)):
        held[step] = group[...]
    for i in range(NX):
        step = (2 * y - i + NX) % NX
        heads = jnp.concatenate([held[step, j] for j in range(NH * NZ1)], axis=1)
        copies[i].wait()
        for k in range(NK):
            for b in range(2):
                columns = [parts[i, k, 2 * h + b].reshape(2 * HEAD, 256) for h in range(NH)]
                term = jnp.dot(
                    heads, jnp.concatenate(columns, axis=0), preferred_element_type=jnp.float32
                )
                lanes = slice(b * 256, b * 256 + 256)
                if i == 0:
                    acc[k, :, lanes] = term
                else:
                    acc[k, :, lanes] += term
    rows = mine_ref.shape[0]
    near_rows = pl.ds(pl.multiple_of(z0 * rows, rows), rows)
    far_rows = pl.ds(pl.multiple_of((1 - z0) * rows, rows), rows)
    for b in range(2):
        for k in range(NK):
            lo = (2 * b + k) * 256
            lanes = slice(b * 256, b * 256 + 256)
            mine_ref[:, lo : lo + 256] = acc[k, near_rows, lanes]
            other_ref[:, lo : lo + 256] = acc[k, far_rows, lanes].astype(jnp.bfloat16)


def per_device(hyena_feats, short_taps, decay_rate, residue, attn_qkv, out_weight):
    rows, width = hyena_feats.shape[1:]
    x, k, y = lax.axis_index("x"), lax.axis_index("k"), lax.axis_index("y")
    z1, z0 = lax.axis_index("z1"), lax.axis_index("z0")
    swap = [(0, 1), (1, 0)]
    short = jax.ShapeDtypeStruct
    bf16, f32 = jnp.bfloat16, jnp.float32
    dma = pltpu.SemaphoreType.DMA

    tail = local_call(
        tail_kernel,
        short((3, 2, width), f32),
        (SLOW,),
        "tail",
        10**8,
        (pltpu.VMEM((3, 16, width), bf16), dma((1,))),
    )(hyena_feats)
    packed = local_call(
        pack_kernel,
        short((NZ, 3, rows, HEAD), bf16),
        (SLOW,),
        "pack",
        10**8,
        (dma((3 * NZ,)),),
        after=(tail,),
    )(attn_qkv)
    qkv = lax.all_to_all(packed, ("z1", "z0"), 0, 0)
    halo = lax.ppermute(tail, ALL, moved(next_ctx))
    plane = short((rows, width), f32)
    poles = short(decay_rate.shape, f32)
    ends, prod, gate_rows, rate = local_call(
        ends_kernel,
        (short((2, rows, HEAD), bf16), plane, plane, poles),
        (SLOW, FAST, SLOW, SLOW),
        "ends",
        10**9,
        (
            pltpu.VMEM((3, rows, width), bf16),
            pltpu.VMEM(short_taps.shape, f32),
            pltpu.VMEM((3, rows + 8, width), f32),
            dma((3,)),
        ),
    )(hyena_feats, halo, short_taps, decay_rate)
    moved_weight = lax.ppermute(out_weight, ALL, moved(place_weight))
    spread = local_call(
        spread_kernel,
        short((NX, 2 * NZ + 2, rows, HEAD), bf16),
        (FAST, FAST),
        "spread",
        10**8,
        after=(moved_weight,),
    )(qkv, ends)
    far_own = lax.all_to_all(spread, "x", 0, 0)
    far_other = lax.ppermute(far_own, "k", swap)

    z = (2 * z1 + z0).reshape(1)
    half = short((NZ1, HEAD, out_weight.shape[1]), bf16)
    same, opposite = local_call(
        halves_kernel, (half, half), (SMEM, FAST), "halves", 10**8, after=(spread,)
    )(z, moved_weight)
    arrived = [same] + [
        lax.ppermute(opposite if steps % 2 else same, ALL, along_z(steps)) for steps in (1, 2, 3)
    ]
    placed = local_call(
        stack_kernel, short((NZ, *half.shape), bf16), (SMEM,) + (FAST,) * NZ, "stack", 10**8,
        after=(far_own,),
    )(z, *arrived)
    weight = lax.all_gather(placed, ("x", "k")).reshape(NX, NK, *placed.shape)

    where = jnp.stack([x, k])
    line = short((1, NZ * rows), f32)
    square = short((HEAD, NZ * rows), f32)
    partial = local_call(
        own_kernel, (line, line, square), (SMEM, FAST, FAST), "own", 2 * 10**9
    )(where, qkv, far_own)
    attended = local_call(
        other_kernel,
        short((NH, NZ1, NZ0 * rows, HEAD), bf16),
        (SMEM,) + (FAST,) * 5,
        "other",
        2 * 10**9,
        [pltpu.VMEM(part.shape, f32) for part in (line, line, square)],
    )(where, qkv, *partial, far_other)
    rate = gate(rate, attended)
    group = lax.all_to_all(attended.reshape(NH * NZ1, NZ0 * rows, HEAD), ("h", "z1"), 0, 0)
    groups = [group] + [
        lax.ppermute(group, "y", [(i, (i + step) % NY) for i in range(NY)]) for step in (1, 3, 2)
    ]

    parts = local_call(
        combine_kernel,
        short((NZ, *poles.shape), f32),
        (SMEM, FAST, FAST, FAST),
        "combine",
        10**8,
        (pltpu.VMEM((NX, NK, *poles.shape), f32),),
        after=(group,),
    )(jnp.stack([x, 2 * z1 + z0, k]), rate, far_own, far_other)
    parts = lax.all_to_all(parts, ("z1", "z0"), 0, 0)

    mine, other = local_call(
        project_kernel,
        (short((rows, width), f32), short((rows, width), bf16)),
        (SMEM,) + (FAST,) * 4 + (SLOW,),
        "project",
        2 * 10**9,
        (
            pltpu.VMEM((NY, *group.shape), bf16),
            pltpu.VMEM(weight.shape, bf16),
            pltpu.VMEM((NK, NZ0 * rows, width // 2), f32),
            dma((NX,)),
        ),
    )(jnp.stack([y, z0]), *groups, weight)
    received = lax.ppermute(other, "z0", swap)

    rho = residue * jnp.sqrt(-jnp.expm1(-2.0 * rate) / rate.shape[0])
    hyena_mixed = local_call(
        mix_kernel,
        short((rows, width), bf16),
        (FAST,) * 5,
        "mix",
        4 * 10**9,
    )(rate, rho, parts, prod, gate_rows)
    return hyena_mixed, (mine + received.astype(f32)).astype(bf16)


def solution(mesh):
    fine = Mesh(mesh.devices.reshape(NX, NZ1, NZ0, NK, NY, NH), ALL)
    ctx, tp = ("x", "z1", "z0", "k"), ("y", "h")
    return jax.shard_map(
        per_device,
        mesh=fine,
        in_specs=(
            P(None, ctx, tp),
            P(None, None, tp),
            P(None, tp),
            P(None, tp),
            P(None, ctx, tp),
            P(tp, ctx),
        ),
        out_specs=(P(ctx, tp), P(ctx, tp)),
        check_vma=False,
    )
```

```python
import math

import jax
import jax.numpy as jnp
from jax import lax
from jax.experimental import pallas as pl
from jax.experimental.pallas import tpu as pltpu
from jax.sharding import Mesh, PartitionSpec as P

HEAD = 128
NX, NZ1, NZ0, NK, NY, NH = 4, 2, 2, 2, 4, 2
NZ = NZ1 * NZ0
ALL = ("x", "z1", "z0", "k", "y", "h")
SIZES = dict(x=NX, z1=NZ1, z0=NZ0, k=NK, y=NY, h=NH)
SCALE = math.log2(math.e) / math.sqrt(HEAD)
VMEM = 48 * 1024 * 1024


def linear(**c):
    index = 0
    for name in ALL:
        index = index * SIZES[name] + c[name]
    return index


def places():
    for index in range(256):
        rest, c = index, {}
        for name in reversed(ALL):
            c[name] = rest % SIZES[name]
            rest //= SIZES[name]
        yield c


def moved(change):
    pairs = []
    for c in places():
        d = change(**c)
        if d is not None:
            pairs.append((linear(**c), linear(**dict(c, **d))))
    return pairs


def next_ctx(x, z1, z0, k, **_):
    place = ((x * NZ1 + z1) * NZ0 + z0) * NK + k + 1
    if place == NX * NZ * NK:
        return None
    return dict(x=place // (NZ * NK), z1=place // 4 % 2, z0=place // 2 % 2, k=place % 2)


def along_z(steps):
    def change(z1, z0, **_):
        z = (2 * z1 + z0 + steps) % NZ
        return dict(z1=z // 2, z0=z % 2)

    return moved(change)


def place_weight(x, z1, z0, k, y, h):
    return dict(x=(x + y) % NX, z1=h, z0=z0, k=k, y=x, h=z1)


SMEM = pl.BlockSpec(memory_space=pltpu.SMEM)
FAST = pl.BlockSpec(memory_space=pltpu.VMEM)
SLOW = pl.BlockSpec(memory_space=pltpu.HBM)
ANY = pl.BlockSpec(memory_space=pl.ANY)


def placed_out(out):
    return FAST if isinstance(out, jax.ShapeDtypeStruct) else SLOW


def local_call(kernel, out_shape, specs, name, flops, scratch=(), after=()):
    count = len(specs)

    def body(*refs):
        kernel(*refs[:count], *refs[count + len(after) :])

    call = pl.pallas_call(
        body,
        out_shape=out_shape,
        in_specs=list(specs) + [ANY] * len(after),
        out_specs=jax.tree.map(placed_out, out_shape),
        scratch_shapes=list(scratch),
        compiler_params=pltpu.CompilerParams(vmem_limit_bytes=VMEM),
        cost_estimate=pl.CostEstimate(flops=flops, bytes_accessed=2_000_000, transcendentals=0),
        name=name,
    )

    def placed(operand, spec):
        return pltpu.with_memory_space_constraint(operand, pltpu.HBM) if spec is SLOW else operand

    return lambda *operands: call(*map(placed, operands, specs), *after)


def gate(value, *after):
    return pl.pallas_call(
        lambda *refs: None,
        out_shape=jax.ShapeDtypeStruct(value.shape, value.dtype),
        in_specs=[ANY] * (1 + len(after)),
        out_specs=ANY,
        input_output_aliases={0: 0},
        name="gate",
    )(value, *after)


def started(sems, pairs):
    copies = [pltpu.make_async_copy(a, b, sems.at[i]) for i, (a, b) in enumerate(pairs)]
    for copy in copies:
        copy.start()
    return copies


def finished(copies):
    for copy in copies:
        copy.wait()


def fill_ext(x, halo_ref, ext, streams):
    for slot, stream in enumerate(streams):
        ext[slot, 6:8] = halo_ref[stream]
        for lo in range(0, x.shape[1], 32):
            ext[slot, lo + 8 : lo + 40] = x[slot, lo : lo + 32].astype(jnp.float32)


def featured_rows(ext, taps_ref, slot, stream, lo, rows):
    taps = taps_ref[stream]
    total = taps[0:1] * ext[slot, lo + 8 : lo + 8 + rows]
    for j in (1, 2):
        total += taps[j : j + 1] * ext[slot, lo + 8 - j : lo + 8 - j + rows]
    return total


def ends_kernel(
    feats, halo_ref, taps_hbm, decay_hbm, out_ref, prod_hbm, gate_hbm, rate_hbm,
    x, taps, rate, prod, gate_rows, ext, sems, out_sems,
):
    finished(started(sems, ((feats, x), (taps_hbm, taps), (decay_hbm, rate))))
    rows, order = x.shape[1], rate.shape[0]
    fill_ext(x, halo_ref, ext, (0, 1, 2))
    for lo in range(0, rows, 16):
        gate_rows[lo : lo + 16] = featured_rows(ext, taps, 0, 0, lo, 16)
        first = featured_rows(ext, taps, 1, 1, lo, 16)
        prod[lo : lo + 16] = first * featured_rows(ext, taps, 2, 2, lo, 16)
    written = started(out_sems, ((prod, prod_hbm), (gate_rows, gate_hbm), (rate, rate_hbm)))
    decay = jnp.exp(-rate[...])

    def body(i, state):
        block = prod[pl.ds(pl.multiple_of(i * 8, 8), 8), :]
        for j in range(8):
            state = decay * state + block[j : j + 1]
        return state

    state = lax.fori_loop(0, rows // 8, body, jnp.zeros(rate.shape, jnp.float32))
    for j in range(state.shape[1] // HEAD):
        block = state[:, j * HEAD : (j + 1) * HEAD]
        high = block.astype(jnp.bfloat16)
        out_ref[0, j * order : (j + 1) * order] = high
        out_ref[1, j * order : (j + 1) * order] = (block - high.astype(jnp.float32)).astype(
            jnp.bfloat16
        )
    finished(written)


def combine_kernel(place_ref, rate_hbm, own_ref, other_ref, out_ref, rate_ref, ends, sems):
    finished(started(sems, ((rate_hbm, rate_ref),)))
    x, z, k = place_ref[0], place_ref[1], place_ref[2]
    rate = rate_ref[...]
    order = rate.shape[0]

    def over(blocks):
        return jnp.exp(rate * (-128.0 * jnp.maximum(blocks, 0).astype(jnp.float32)))

    for row in range(NX):
        for side, ref in enumerate((own_ref, other_ref)):
            both = ref[row, 2 * NZ].astype(jnp.float32) + ref[row, 2 * NZ + 1].astype(jnp.float32)
            for j in range(rate.shape[1] // HEAD):
                lanes = slice(j * HEAD, (j + 1) * HEAD)
                ends[row, side, :, lanes] = both[j * order : (j + 1) * order]

    def end_of(row, core):
        return ends[row, jnp.where(k == core, 0, 1)]

    step, across, rest = over(jnp.int32(1)), over(jnp.int32(NZ * NK)), over(NZ * NK - NK * z - NK)
    earlier = jnp.zeros(rate.shape, jnp.float32)
    for row in range(NX - 1):
        whole = rest * (step * end_of(row, 0) + end_of(row, 1))
        earlier = jnp.where(x > row, across * earlier + whole, earlier)
    for target in range(NZ):
        total = over(NK * target + k) * earlier
        for core in range(NK):
            blocks = (NK * target + k) - (NK * z + core) - 1
            total = total + jnp.where(blocks >= 0, over(blocks) * end_of(x, core), 0.0)
        out_ref[target] = total


def mix_kernel(
    rate_hbm, rho_ref, parts_ref, prod_hbm, gate_hbm, out_ref, rate, prod, gate_rows, sems
):
    finished(started(sems, ((rate_hbm, rate), (prod_hbm, prod), (gate_hbm, gate_rows))))
    rows, width = prod.shape
    decay = jnp.exp(-rate[...])
    start = parts_ref[0]
    for z in range(1, NZ):
        start = start + parts_ref[z]
    rho = rho_ref[...]
    sub = lax.broadcasted_iota(jnp.int32, (8, width), 0)

    def body(i, state):
        base = pl.multiple_of(i * 16, 16)
        mixed = []
        for half in range(2):
            block = prod[pl.ds(base + 8 * half, 8), :]
            conv = jnp.zeros((8, width), jnp.float32)
            for j in range(8):
                state = decay * state + block[j : j + 1]
                row = jnp.sum(rho * state, axis=0, keepdims=True)
                conv = jnp.where(sub == j, row, conv)
            mixed.append(conv * gate_rows[pl.ds(base + 8 * half, 8), :])
        out_ref[pl.ds(base, 16), :] = jnp.concatenate(mixed, axis=0).astype(jnp.bfloat16)
        return state

    lax.fori_loop(0, rows // 16, body, start)


def tail_kernel(feats, halo_ref, tail, sems):
    rows = feats.shape[1]
    finished(started(sems, [(feats.at[:, pl.ds(rows - 16, 16), :], tail)]))
    halo_ref[...] = tail[:, 14:16].astype(jnp.float32)


def pack_kernel(qkv, out_ref, sems):
    lanes = [pl.ds(head * HEAD, HEAD) for head in range(NZ)]
    finished(started(sems, [(qkv.at[:, :, lanes[i]], out_ref.at[i]) for i in range(NZ)]))


def halves_kernel(place_ref, weight_ref, same_ref, other_ref):
    for half in range(NZ0):

        @pl.when(place_ref[0] % NZ0 == half)
        def _():
            for ref, z0 in ((same_ref, half), (other_ref, 1 - half)):
                for part in range(NZ1):
                    lo = (2 * part + z0) * HEAD
                    ref[part] = weight_ref[lo : lo + HEAD]


def stack_kernel(place_ref, *refs):
    for steps, ref in enumerate(refs[:-1]):
        refs[-1][(place_ref[0] + NZ - steps) % NZ] = ref[...]


def spread_kernel(qkv_ref, ends_ref, out_ref):
    for z in range(NZ):
        for i in range(out_ref.shape[0]):
            out_ref[i, 2 * z : 2 * z + 2] = qkv_ref[z, 1:]
    for i in range(out_ref.shape[0]):
        out_ref[i, 2 * NZ :] = ends_ref[...]


def folded(q, pairs, top, total, acc, visible=None):
    keys = pairs[:, 0].reshape(-1, HEAD)
    values = pairs[:, 1].reshape(-1, HEAD)
    s = lax.dot_general(keys, q, (((1,), (1,)), ((), ())), preferred_element_type=jnp.float32)
    if visible is not None:
        s = jnp.where(visible, s, -1e30)
    new = jnp.maximum(top, jnp.max(s, axis=0, keepdims=True))
    p = jnp.exp2((s - new) * SCALE)
    again = jnp.exp2((top - new) * SCALE)
    added = jnp.dot(values.T, p.astype(jnp.bfloat16), preferred_element_type=jnp.float32)
    return new, total * again + jnp.sum(p, axis=0, keepdims=True), acc * again + added


def pairs_of(ref, row):
    return ref[row, 0 : 2 * NZ].reshape(NZ, 2, HEAD, HEAD)


def fold_rows(x, q, ref, top, total, acc):
    for row in range(NX - 1):

        @pl.when(x > row)
        def _():
            top[...], total[...], acc[...] = folded(
                q, pairs_of(ref, row), top[...], total[...], acc[...]
            )


def own_kernel(place_ref, qkv_ref, kv_ref, top_ref, total_ref, acc_ref):
    x = place_ref[0]
    rows = NZ * HEAD
    q = qkv_ref[:, 0].reshape(rows, HEAD)
    col = lax.broadcasted_iota(jnp.int32, (1, rows), 1)
    row = lax.broadcasted_iota(jnp.int32, (rows, 1), 0)
    lowest = jnp.full((1, rows), -1e30, jnp.float32)
    nothing = jnp.zeros((1, rows), jnp.float32), jnp.zeros((HEAD, rows), jnp.float32)
    top_ref[...], total_ref[...], acc_ref[...] = folded(
        q, pairs_of(kv_ref, x), lowest, *nothing, row <= col
    )
    fold_rows(x, q, kv_ref, top_ref, total_ref, acc_ref)


def other_kernel(
    place_ref, qkv_ref, top_ref, total_ref, acc_ref, kv_ref, out_ref, top, total, acc
):
    x, k = place_ref[0], place_ref[1]
    rows = NZ * HEAD
    q = qkv_ref[:, 0].reshape(rows, HEAD)
    col = lax.broadcasted_iota(jnp.int32, (1, rows), 1)
    row = lax.broadcasted_iota(jnp.int32, (rows, 1), 0)
    here = (2 * (col // HEAD) + k) * HEAD + col % HEAD
    there = (2 * (row // HEAD) + 1 - k) * HEAD + row % HEAD
    top[...], total[...], acc[...] = folded(
        q, pairs_of(kv_ref, x), top_ref[...], total_ref[...], acc_ref[...], there <= here
    )
    fold_rows(x, q, kv_ref, top, total, acc)
    result = (acc[...] / total[...]).T.astype(jnp.bfloat16).reshape(out_ref.shape[1:])
    for h in range(NH):
        out_ref[h] = result


def project_kernel(place_ref, g0, g1, g2, g3, w_hbm, mine_ref, other_ref, held, parts, acc, sems):
    y, z0 = place_ref[0], place_ref[1]
    copies = started(sems, [(w_hbm.at[i], parts.at[i]) for i in range(NX)])
    for step, group in zip((0, 1, 3, 2), (g0, g1, g2, g3)):
        held[step] = group[...]
    for i in range(NX):
        step = (2 * y - i + NX) % NX
        heads = jnp.concatenate([held[step, j] for j in range(NH * NZ1)], axis=1)
        copies[i].wait()
        for k in range(NK):
            for b in range(2):
                columns = [parts[i, k, 2 * h + b].reshape(2 * HEAD, 256) for h in range(NH)]
                term = jnp.dot(
                    heads, jnp.concatenate(columns, axis=0), preferred_element_type=jnp.float32
                )
                lanes = slice(b * 256, b * 256 + 256)
                if i == 0:
                    acc[k, :, lanes] = term
                else:
                    acc[k, :, lanes] += term
    rows = mine_ref.shape[0]
    near_rows = pl.ds(pl.multiple_of(z0 * rows, rows), rows)
    far_rows = pl.ds(pl.multiple_of((1 - z0) * rows, rows), rows)
    for b in range(2):
        for k in range(NK):
            lo = (2 * b + k) * 256
            lanes = slice(b * 256, b * 256 + 256)
            mine_ref[:, lo : lo + 256] = acc[k, near_rows, lanes]
            other_ref[:, lo : lo + 256] = acc[k, far_rows, lanes].astype(jnp.bfloat16)


def per_device(hyena_feats, short_taps, decay_rate, residue, attn_qkv, out_weight):
    rows, width = hyena_feats.shape[1:]
    x, k, y = lax.axis_index("x"), lax.axis_index("k"), lax.axis_index("y")
    z1, z0 = lax.axis_index("z1"), lax.axis_index("z0")
    swap = [(0, 1), (1, 0)]
    short = jax.ShapeDtypeStruct
    bf16, f32 = jnp.bfloat16, jnp.float32
    dma = pltpu.SemaphoreType.DMA

    tail = local_call(
        tail_kernel,
        short((3, 2, width), f32),
        (SLOW,),
        "tail",
        10**8,
        (pltpu.VMEM((3, 16, width), bf16), dma((1,))),
    )(hyena_feats)
    packed = local_call(
        pack_kernel,
        short((NZ, 3, rows, HEAD), bf16),
        (SLOW,),
        "pack",
        10**8,
        (dma((NZ,)),),
        after=(tail,),
    )(attn_qkv)
    halo = lax.ppermute(tail, ALL, moved(next_ctx))
    qkv = lax.all_to_all(gate(packed, halo), ("z1", "z0"), 0, 0)
    plane = short((rows, width), f32)
    poles = short(decay_rate.shape, f32)
    ends, prod, gate_rows, rate = local_call(
        ends_kernel,
        (
            short((2, rows, HEAD), bf16),
            pltpu.HBM(plane.shape, f32),
            pltpu.HBM(plane.shape, f32),
            pltpu.HBM(poles.shape, f32),
        ),
        (SLOW, FAST, SLOW, SLOW),
        "ends",
        10**9,
        (
            pltpu.VMEM((3, rows, width), bf16),
            pltpu.VMEM(short_taps.shape, f32),
            pltpu.VMEM(poles.shape, f32),
            pltpu.VMEM(plane.shape, f32),
            pltpu.VMEM(plane.shape, f32),
            pltpu.VMEM((3, rows + 8, width), f32),
            dma((3,)),
            dma((3,)),
        ),
    )(hyena_feats, halo, short_taps, decay_rate)
    moved_weight = lax.ppermute(out_weight, ALL, moved(place_weight))
    spread = local_call(
        spread_kernel,
        short((NX, 2 * NZ + 2, rows, HEAD), bf16),
        (FAST, FAST),
        "spread",
        10**8,
        after=(moved_weight,),
    )(qkv, ends)
    far_own = lax.all_to_all(spread, "x", 0, 0)
    far_other = lax.ppermute(far_own, "k", swap)

    z = (2 * z1 + z0).reshape(1)
    half = short((NZ1, HEAD, out_weight.shape[1]), bf16)
    same, opposite = local_call(
        halves_kernel, (half, half), (SMEM, FAST), "halves", 10**8, after=(spread,)
    )(z, moved_weight)
    arrived = [same] + [
        lax.ppermute(opposite if steps % 2 else same, ALL, along_z(steps)) for steps in (1, 2, 3)
    ]
    placed = local_call(
        stack_kernel, short((NZ, *half.shape), bf16), (SMEM,) + (FAST,) * NZ, "stack", 10**8,
        after=(far_own,),
    )(z, *arrived)
    weight = lax.all_gather(placed, ("x", "k")).reshape(NX, NK, *placed.shape)

    where = jnp.stack([x, k])
    line = short((1, NZ * rows), f32)
    square = short((HEAD, NZ * rows), f32)
    partial = local_call(
        own_kernel, (line, line, square), (SMEM, FAST, FAST), "own", 2 * 10**9
    )(where, qkv, far_own)
    attended = local_call(
        other_kernel,
        short((NH, NZ1, NZ0 * rows, HEAD), bf16),
        (SMEM,) + (FAST,) * 5,
        "other",
        2 * 10**9,
        [pltpu.VMEM(part.shape, f32) for part in (line, line, square)],
    )(where, qkv, *partial, far_other)
    group = lax.all_to_all(attended.reshape(NH * NZ1, NZ0 * rows, HEAD), ("h", "z1"), 0, 0)
    groups = [group] + [
        lax.ppermute(group, "y", [(i, (i + step) % NY) for i in range(NY)]) for step in (1, 3, 2)
    ]

    parts = local_call(
        combine_kernel,
        short((NZ, *poles.shape), f32),
        (SMEM, SLOW, FAST, FAST),
        "combine",
        10**8,
        (pltpu.VMEM(poles.shape, f32), pltpu.VMEM((NX, NK, *poles.shape), f32), dma((1,))),
        after=(group,),
    )(jnp.stack([x, 2 * z1 + z0, k]), decay_rate, far_own, far_other)
    parts = lax.all_to_all(parts, ("z1", "z0"), 0, 0)

    mine, other = local_call(
        project_kernel,
        (short((rows, width), f32), short((rows, width), bf16)),
        (SMEM,) + (FAST,) * 4 + (SLOW,),
        "project",
        2 * 10**9,
        (
            pltpu.VMEM((NY, *group.shape), bf16),
            pltpu.VMEM(weight.shape, bf16),
            pltpu.VMEM((NK, NZ0 * rows, width // 2), f32),
            dma((NX,)),
        ),
    )(jnp.stack([y, z0]), *groups, weight)
    received = lax.ppermute(other, "z0", swap)

    rho = residue * jnp.sqrt(-jnp.expm1(-2.0 * rate) / rate.shape[0])
    hyena_mixed = local_call(
        mix_kernel,
        short((rows, width), bf16),
        (SLOW, FAST, FAST, SLOW, SLOW),
        "mix",
        4 * 10**9,
        (
            pltpu.VMEM(poles.shape, f32),
            pltpu.VMEM(plane.shape, f32),
            pltpu.VMEM(plane.shape, f32),
            dma((3,)),
        ),
    )(decay_rate, rho, parts, prod, gate_rows)
    return hyena_mixed, (mine + received.astype(f32)).astype(bf16)


def solution(mesh):
    fine = Mesh(mesh.devices.reshape(NX, NZ1, NZ0, NK, NY, NH), ALL)
    ctx, tp = ("x", "z1", "z0", "k"), ("y", "h")
    return jax.shard_map(
        per_device,
        mesh=fine,
        in_specs=(
            P(None, ctx, tp),
            P(None, None, tp),
            P(None, tp),
            P(None, tp),
            P(None, ctx, tp),
            P(tp, ctx),
        ),
        out_specs=(P(ctx, tp), P(ctx, tp)),
        check_vma=False,
    )
```

```python
import math

import jax
import jax.numpy as jnp
from jax import lax
from jax.experimental import pallas as pl
from jax.experimental.pallas import tpu as pltpu
from jax.sharding import Mesh, PartitionSpec as P

HEAD = 128
NX, NZ1, NZ0, NK, NY, NH = 4, 2, 2, 2, 4, 2
NZ = NZ1 * NZ0
ALL = ("x", "z1", "z0", "k", "y", "h")
SIZES = dict(x=NX, z1=NZ1, z0=NZ0, k=NK, y=NY, h=NH)
SCALE = math.log2(math.e) / math.sqrt(HEAD)
VMEM = 48 * 1024 * 1024


def linear(**c):
    index = 0
    for name in ALL:
        index = index * SIZES[name] + c[name]
    return index


def places():
    for index in range(256):
        rest, c = index, {}
        for name in reversed(ALL):
            c[name] = rest % SIZES[name]
            rest //= SIZES[name]
        yield c


def moved(change):
    pairs = []
    for c in places():
        d = change(**c)
        if d is not None:
            pairs.append((linear(**c), linear(**dict(c, **d))))
    return pairs


def next_ctx(x, z1, z0, k, **_):
    place = ((x * NZ1 + z1) * NZ0 + z0) * NK + k + 1
    if place == NX * NZ * NK:
        return None
    return dict(x=place // (NZ * NK), z1=place // 4 % 2, z0=place // 2 % 2, k=place % 2)


def along_z(steps):
    def change(z1, z0, **_):
        z = (2 * z1 + z0 + steps) % NZ
        return dict(z1=z // 2, z0=z % 2)

    return moved(change)


def place_weight(x, z1, z0, k, y, h):
    return dict(x=(x + y) % NX, z1=h, z0=z0, k=k, y=x, h=z1)


SMEM = pl.BlockSpec(memory_space=pltpu.SMEM)
FAST = pl.BlockSpec(memory_space=pltpu.VMEM)
SLOW = pl.BlockSpec(memory_space=pltpu.HBM)
ANY = pl.BlockSpec(memory_space=pl.ANY)


def placed_out(out):
    return FAST if isinstance(out, jax.ShapeDtypeStruct) else SLOW


def local_call(kernel, out_shape, specs, name, flops, scratch=(), after=()):
    count = len(specs)

    def body(*refs):
        kernel(*refs[:count], *refs[count + len(after) :])

    call = pl.pallas_call(
        body,
        out_shape=out_shape,
        in_specs=list(specs) + [ANY] * len(after),
        out_specs=jax.tree.map(placed_out, out_shape),
        scratch_shapes=list(scratch),
        compiler_params=pltpu.CompilerParams(vmem_limit_bytes=VMEM),
        cost_estimate=pl.CostEstimate(flops=flops, bytes_accessed=2_000_000, transcendentals=0),
        name=name,
    )

    def placed(operand, spec):
        return pltpu.with_memory_space_constraint(operand, pltpu.HBM) if spec is SLOW else operand

    return lambda *operands: call(*map(placed, operands, specs), *after)


def gate(value, *after):
    return pl.pallas_call(
        lambda *refs: None,
        out_shape=jax.ShapeDtypeStruct(value.shape, value.dtype),
        in_specs=[ANY] * (1 + len(after)),
        out_specs=ANY,
        input_output_aliases={0: 0},
        name="gate",
    )(value, *after)


def started(sems, pairs):
    copies = [pltpu.make_async_copy(a, b, sems.at[i]) for i, (a, b) in enumerate(pairs)]
    for copy in copies:
        copy.start()
    return copies


def finished(copies):
    for copy in copies:
        copy.wait()


def fill_ext(x, halo_ref, ext, streams):
    for slot, stream in enumerate(streams):
        ext[slot, 6:8] = halo_ref[stream]
        for lo in range(0, x.shape[1], 32):
            ext[slot, lo + 8 : lo + 40] = x[slot, lo : lo + 32].astype(jnp.float32)


def featured_rows(ext, taps_ref, slot, stream, lo, rows):
    taps = taps_ref[stream]
    total = taps[0:1] * ext[slot, lo + 8 : lo + 8 + rows]
    for j in (1, 2):
        total += taps[j : j + 1] * ext[slot, lo + 8 - j : lo + 8 - j + rows]
    return total


def ends_kernel(
    feats, halo_ref, taps_hbm, decay_hbm, out_ref, prod_hbm, gate_hbm,
    x, taps, rate, prod, gate_rows, ext, sems, out_sems,
):
    finished(started(sems, ((feats, x), (taps_hbm, taps), (decay_hbm, rate))))
    rows, order = x.shape[1], rate.shape[0]
    fill_ext(x, halo_ref, ext, (0, 1, 2))
    for lo in range(0, rows, 16):
        gate_rows[lo : lo + 16] = featured_rows(ext, taps, 0, 0, lo, 16)
        first = featured_rows(ext, taps, 1, 1, lo, 16)
        prod[lo : lo + 16] = first * featured_rows(ext, taps, 2, 2, lo, 16)
    written = started(out_sems, ((prod, prod_hbm), (gate_rows, gate_hbm)))
    decay = jnp.exp(-rate[...])

    def body(i, state):
        block = prod[pl.ds(pl.multiple_of(i * 8, 8), 8), :]
        for j in range(8):
            state = decay * state + block[j : j + 1]
        return state

    state = lax.fori_loop(0, rows // 8, body, jnp.zeros(rate.shape, jnp.float32))
    for j in range(state.shape[1] // HEAD):
        block = state[:, j * HEAD : (j + 1) * HEAD]
        high = block.astype(jnp.bfloat16)
        out_ref[0, j * order : (j + 1) * order] = high
        out_ref[1, j * order : (j + 1) * order] = (block - high.astype(jnp.float32)).astype(
            jnp.bfloat16
        )
    finished(written)


def combine_kernel(place_ref, rate_hbm, own_ref, other_ref, out_ref, rate_ref, ends, sems):
    finished(started(sems, ((rate_hbm, rate_ref),)))
    x, z, k = place_ref[0], place_ref[1], place_ref[2]
    rate = rate_ref[...]
    order = rate.shape[0]

    def over(blocks):
        return jnp.exp(rate * (-128.0 * jnp.maximum(blocks, 0).astype(jnp.float32)))

    for row in range(NX):
        for side, ref in enumerate((own_ref, other_ref)):
            both = ref[row, 2 * NZ].astype(jnp.float32) + ref[row, 2 * NZ + 1].astype(jnp.float32)
            for j in range(rate.shape[1] // HEAD):
                lanes = slice(j * HEAD, (j + 1) * HEAD)
                ends[row, side, :, lanes] = both[j * order : (j + 1) * order]

    def end_of(row, core):
        return ends[row, jnp.where(k == core, 0, 1)]

    step, across, rest = over(jnp.int32(1)), over(jnp.int32(NZ * NK)), over(NZ * NK - NK * z - NK)
    earlier = jnp.zeros(rate.shape, jnp.float32)
    for row in range(NX - 1):
        whole = rest * (step * end_of(row, 0) + end_of(row, 1))
        earlier = jnp.where(x > row, across * earlier + whole, earlier)
    for target in range(NZ):
        total = over(NK * target + k) * earlier
        for core in range(NK):
            blocks = (NK * target + k) - (NK * z + core) - 1
            total = total + jnp.where(blocks >= 0, over(blocks) * end_of(x, core), 0.0)
        out_ref[target] = total


def one_less_exp(y):
    series = 1.0 - y / 9.0
    for n in range(8, 1, -1):
        series = 1.0 - y / n * series
    return jnp.where(y < 0.5, y * series, 1.0 - jnp.exp(-y))


def mix_kernel(
    rate_hbm, residue_hbm, parts_ref, prod_hbm, gate_hbm, out_ref,
    rate, residue, prod, gate_rows, sems,
):
    pairs = ((rate_hbm, rate), (residue_hbm, residue), (prod_hbm, prod), (gate_hbm, gate_rows))
    finished(started(sems, pairs))
    rows, width = prod.shape
    decay = jnp.exp(-rate[...])
    start = parts_ref[0]
    for z in range(1, NZ):
        start = start + parts_ref[z]
    rho = residue[...] * jnp.sqrt(one_less_exp(2.0 * rate[...]) / rate.shape[0])
    sub = lax.broadcasted_iota(jnp.int32, (8, width), 0)

    def body(i, state):
        base = pl.multiple_of(i * 16, 16)
        mixed = []
        for half in range(2):
            block = prod[pl.ds(base + 8 * half, 8), :]
            conv = jnp.zeros((8, width), jnp.float32)
            for j in range(8):
                state = decay * state + block[j : j + 1]
                row = jnp.sum(rho * state, axis=0, keepdims=True)
                conv = jnp.where(sub == j, row, conv)
            mixed.append(conv * gate_rows[pl.ds(base + 8 * half, 8), :])
        out_ref[pl.ds(base, 16), :] = jnp.concatenate(mixed, axis=0).astype(jnp.bfloat16)
        return state

    lax.fori_loop(0, rows // 16, body, start)


def pack_kernel(qkv, feats, out_ref, halo_ref, tail, sems):
    rows = qkv.shape[1]
    lanes = [pl.ds(head * HEAD, HEAD) for head in range(NZ)]
    pairs = [(qkv.at[:, :, lanes[i]], out_ref.at[i]) for i in range(NZ)]
    pairs.append((feats.at[:, pl.ds(rows - 16, 16), :], tail))
    finished(started(sems, pairs))
    halo_ref[...] = tail[:, 14:16].astype(jnp.float32)


def halves_kernel(place_ref, weight_ref, same_ref, other_ref):
    for half in range(NZ0):

        @pl.when(place_ref[0] % NZ0 == half)
        def _():
            for ref, z0 in ((same_ref, half), (other_ref, 1 - half)):
                for part in range(NZ1):
                    lo = (2 * part + z0) * HEAD
                    ref[part] = weight_ref[lo : lo + HEAD]


def stack_kernel(place_ref, *refs):
    for steps, ref in enumerate(refs[:-1]):
        refs[-1][(place_ref[0] + NZ - steps) % NZ] = ref[...]


def spread_kernel(qkv_ref, ends_ref, out_ref):
    for z in range(NZ):
        for i in range(out_ref.shape[0]):
            out_ref[i, 2 * z : 2 * z + 2] = qkv_ref[z, 1:]
    for i in range(out_ref.shape[0]):
        out_ref[i, 2 * NZ :] = ends_ref[...]


def folded(q, pairs, top, total, acc, visible=None):
    keys = pairs[:, 0].reshape(-1, HEAD)
    values = pairs[:, 1].reshape(-1, HEAD)
    s = lax.dot_general(keys, q, (((1,), (1,)), ((), ())), preferred_element_type=jnp.float32)
    if visible is not None:
        s = jnp.where(visible, s, -1e30)
    new = jnp.maximum(top, jnp.max(s, axis=0, keepdims=True))
    p = jnp.exp2((s - new) * SCALE)
    again = jnp.exp2((top - new) * SCALE)
    added = jnp.dot(values.T, p.astype(jnp.bfloat16), preferred_element_type=jnp.float32)
    return new, total * again + jnp.sum(p, axis=0, keepdims=True), acc * again + added


def pairs_of(ref, row):
    return ref[row, 0 : 2 * NZ].reshape(NZ, 2, HEAD, HEAD)


def fold_rows(x, q, ref, top, total, acc):
    for row in range(NX - 1):

        @pl.when(x > row)
        def _():
            top[...], total[...], acc[...] = folded(
                q, pairs_of(ref, row), top[...], total[...], acc[...]
            )


def own_kernel(place_ref, qkv_ref, kv_ref, top_ref, total_ref, acc_ref):
    x = place_ref[0]
    rows = NZ * HEAD
    q = qkv_ref[:, 0].reshape(rows, HEAD)
    col = lax.broadcasted_iota(jnp.int32, (1, rows), 1)
    row = lax.broadcasted_iota(jnp.int32, (rows, 1), 0)
    lowest = jnp.full((1, rows), -1e30, jnp.float32)
    nothing = jnp.zeros((1, rows), jnp.float32), jnp.zeros((HEAD, rows), jnp.float32)
    top_ref[...], total_ref[...], acc_ref[...] = folded(
        q, pairs_of(kv_ref, x), lowest, *nothing, row <= col
    )
    fold_rows(x, q, kv_ref, top_ref, total_ref, acc_ref)


def other_kernel(
    place_ref, qkv_ref, top_ref, total_ref, acc_ref, kv_ref, out_ref, top, total, acc
):
    x, k = place_ref[0], place_ref[1]
    rows = NZ * HEAD
    q = qkv_ref[:, 0].reshape(rows, HEAD)
    col = lax.broadcasted_iota(jnp.int32, (1, rows), 1)
    row = lax.broadcasted_iota(jnp.int32, (rows, 1), 0)
    here = (2 * (col // HEAD) + k) * HEAD + col % HEAD
    there = (2 * (row // HEAD) + 1 - k) * HEAD + row % HEAD
    top[...], total[...], acc[...] = folded(
        q, pairs_of(kv_ref, x), top_ref[...], total_ref[...], acc_ref[...], there <= here
    )
    fold_rows(x, q, kv_ref, top, total, acc)
    result = (acc[...] / total[...]).T.astype(jnp.bfloat16).reshape(out_ref.shape[1:])
    for h in range(NH):
        out_ref[h] = result


def project_kernel(place_ref, g0, g1, g2, g3, w_hbm, mine_ref, other_ref, held, parts, acc, sems):
    y, z0 = place_ref[0], place_ref[1]
    copies = started(sems, [(w_hbm.at[i], parts.at[i]) for i in range(NX)])
    for step, group in zip((0, 1, 3, 2), (g0, g1, g2, g3)):
        held[step] = group[...]
    for i in range(NX):
        step = (2 * y - i + NX) % NX
        heads = jnp.concatenate([held[step, j] for j in range(NH * NZ1)], axis=1)
        copies[i].wait()
        for k in range(NK):
            for b in range(2):
                columns = [parts[i, k, 2 * h + b].reshape(2 * HEAD, 256) for h in range(NH)]
                term = jnp.dot(
                    heads, jnp.concatenate(columns, axis=0), preferred_element_type=jnp.float32
                )
                lanes = slice(b * 256, b * 256 + 256)
                if i == 0:
                    acc[k, :, lanes] = term
                else:
                    acc[k, :, lanes] += term
    rows = mine_ref.shape[0]
    near_rows = pl.ds(pl.multiple_of(z0 * rows, rows), rows)
    far_rows = pl.ds(pl.multiple_of((1 - z0) * rows, rows), rows)
    for b in range(2):
        for k in range(NK):
            lo = (2 * b + k) * 256
            lanes = slice(b * 256, b * 256 + 256)
            mine_ref[:, lo : lo + 256] = acc[k, near_rows, lanes]
            other_ref[:, lo : lo + 256] = acc[k, far_rows, lanes].astype(jnp.bfloat16)


def per_device(hyena_feats, short_taps, decay_rate, residue, attn_qkv, out_weight):
    rows, width = hyena_feats.shape[1:]
    x, k, y = lax.axis_index("x"), lax.axis_index("k"), lax.axis_index("y")
    z1, z0 = lax.axis_index("z1"), lax.axis_index("z0")
    swap = [(0, 1), (1, 0)]
    short = jax.ShapeDtypeStruct
    bf16, f32 = jnp.bfloat16, jnp.float32
    dma = pltpu.SemaphoreType.DMA

    packed, tail = local_call(
        pack_kernel,
        (short((NZ, 3, rows, HEAD), bf16), short((3, 2, width), f32)),
        (SLOW, SLOW),
        "pack",
        10**8,
        (pltpu.VMEM((3, 16, width), bf16), dma((1 + NZ,))),
    )(attn_qkv, hyena_feats)
    qkv = lax.all_to_all(packed, ("z1", "z0"), 0, 0)
    halo = lax.ppermute(tail, ALL, moved(next_ctx))
    plane = short((rows, width), f32)
    poles = short(decay_rate.shape, f32)
    ends, prod, gate_rows = local_call(
        ends_kernel,
        (
            short((2, rows, HEAD), bf16),
            pltpu.HBM(plane.shape, f32),
            pltpu.HBM(plane.shape, f32),
        ),
        (SLOW, FAST, SLOW, SLOW),
        "ends",
        10**9,
        (
            pltpu.VMEM((3, rows, width), bf16),
            pltpu.VMEM(short_taps.shape, f32),
            pltpu.VMEM(poles.shape, f32),
            pltpu.VMEM(plane.shape, f32),
            pltpu.VMEM(plane.shape, f32),
            pltpu.VMEM((3, rows + 8, width), f32),
            dma((3,)),
            dma((2,)),
        ),
    )(hyena_feats, halo, short_taps, decay_rate)
    moved_weight = lax.ppermute(out_weight, ALL, moved(place_weight))
    spread = local_call(
        spread_kernel,
        short((NX, 2 * NZ + 2, rows, HEAD), bf16),
        (FAST, FAST),
        "spread",
        10**8,
        after=(moved_weight,),
    )(qkv, ends)
    far_own = lax.all_to_all(spread, "x", 0, 0)
    far_other = lax.ppermute(far_own, "k", swap)

    z = (2 * z1 + z0).reshape(1)
    half = short((NZ1, HEAD, out_weight.shape[1]), bf16)
    same, opposite = local_call(
        halves_kernel, (half, half), (SMEM, FAST), "halves", 10**8, after=(spread,)
    )(z, moved_weight)
    arrived = [same] + [
        lax.ppermute(opposite if steps % 2 else same, ALL, along_z(steps)) for steps in (1, 2, 3)
    ]
    placed = local_call(
        stack_kernel, short((NZ, *half.shape), bf16), (SMEM,) + (FAST,) * NZ, "stack", 10**8,
        after=(far_own,),
    )(z, *arrived)
    weight = lax.all_gather(placed, ("x", "k")).reshape(NX, NK, *placed.shape)

    where = jnp.stack([x, k])
    line = short((1, NZ * rows), f32)
    square = short((HEAD, NZ * rows), f32)
    partial = local_call(
        own_kernel, (line, line, square), (SMEM, FAST, FAST), "own", 2 * 10**9
    )(where, qkv, far_own)
    attended = local_call(
        other_kernel,
        short((NH, NZ1, NZ0 * rows, HEAD), bf16),
        (SMEM,) + (FAST,) * 5,
        "other",
        2 * 10**9,
        [pltpu.VMEM(part.shape, f32) for part in (line, line, square)],
    )(where, qkv, *partial, far_other)
    group = lax.all_to_all(attended.reshape(NH * NZ1, NZ0 * rows, HEAD), ("h", "z1"), 0, 0)
    groups = [group] + [
        lax.ppermute(group, "y", [(i, (i + step) % NY) for i in range(NY)]) for step in (1, 3, 2)
    ]

    parts = local_call(
        combine_kernel,
        short((NZ, *poles.shape), f32),
        (SMEM, SLOW, FAST, FAST),
        "combine",
        10**8,
        (pltpu.VMEM(poles.shape, f32), pltpu.VMEM((NX, NK, *poles.shape), f32), dma((1,))),
        after=(group,),
    )(jnp.stack([x, 2 * z1 + z0, k]), decay_rate, far_own, far_other)
    parts = lax.all_to_all(parts, ("z1", "z0"), 0, 0)

    mine, other = local_call(
        project_kernel,
        (short((rows, width), f32), short((rows, width), bf16)),
        (SMEM,) + (FAST,) * 4 + (SLOW,),
        "project",
        2 * 10**9,
        (
            pltpu.VMEM((NY, *group.shape), bf16),
            pltpu.VMEM(weight.shape, bf16),
            pltpu.VMEM((NK, NZ0 * rows, width // 2), f32),
            dma((NX,)),
        ),
    )(jnp.stack([y, z0]), *groups, weight)
    received = lax.ppermute(other, "z0", swap)

    hyena_mixed = local_call(
        mix_kernel,
        short((rows, width), bf16),
        (SLOW, SLOW, FAST, SLOW, SLOW),
        "mix",
        4 * 10**9,
        (
            pltpu.VMEM(poles.shape, f32),
            pltpu.VMEM(poles.shape, f32),
            pltpu.VMEM(plane.shape, f32),
            pltpu.VMEM(plane.shape, f32),
            dma((4,)),
        ),
    )(decay_rate, residue, parts, prod, gate_rows)
    return hyena_mixed, (mine + received.astype(f32)).astype(bf16)


def solution(mesh):
    fine = Mesh(mesh.devices.reshape(NX, NZ1, NZ0, NK, NY, NH), ALL)
    ctx, tp = ("x", "z1", "z0", "k"), ("y", "h")
    return jax.shard_map(
        per_device,
        mesh=fine,
        in_specs=(
            P(None, ctx, tp),
            P(None, None, tp),
            P(None, tp),
            P(None, tp),
            P(None, ctx, tp),
            P(tp, ctx),
        ),
        out_specs=(P(ctx, tp), P(ctx, tp)),
        check_vma=False,
    )
```

```python
import math

import jax
import jax.numpy as jnp
from jax import lax
from jax.experimental import pallas as pl
from jax.experimental.pallas import tpu as pltpu
from jax.sharding import Mesh, PartitionSpec as P

HEAD = 128
NX, NZ1, NZ0, NK, NY, NH = 4, 2, 2, 2, 4, 2
NZ = NZ1 * NZ0
ALL = ("x", "z1", "z0", "k", "y", "h")
SIZES = dict(x=NX, z1=NZ1, z0=NZ0, k=NK, y=NY, h=NH)
SCALE = math.log2(math.e) / math.sqrt(HEAD)
VMEM = 48 * 1024 * 1024


def linear(**c):
    index = 0
    for name in ALL:
        index = index * SIZES[name] + c[name]
    return index


def places():
    for index in range(256):
        rest, c = index, {}
        for name in reversed(ALL):
            c[name] = rest % SIZES[name]
            rest //= SIZES[name]
        yield c


def moved(change):
    pairs = []
    for c in places():
        d = change(**c)
        if d is not None:
            pairs.append((linear(**c), linear(**dict(c, **d))))
    return pairs


def next_ctx(x, z1, z0, k, **_):
    place = ((x * NZ1 + z1) * NZ0 + z0) * NK + k + 1
    if place == NX * NZ * NK:
        return None
    return dict(x=place // (NZ * NK), z1=place // 4 % 2, z0=place // 2 % 2, k=place % 2)


def along_z(steps):
    def change(z1, z0, **_):
        z = (2 * z1 + z0 + steps) % NZ
        return dict(z1=z // 2, z0=z % 2)

    return moved(change)


def place_weight(x, z1, z0, k, y, h):
    return dict(x=(x + y) % NX, z1=h, z0=z0, k=k, y=x, h=z1)


SMEM = pl.BlockSpec(memory_space=pltpu.SMEM)
FAST = pl.BlockSpec(memory_space=pltpu.VMEM)
SLOW = pl.BlockSpec(memory_space=pltpu.HBM)
ANY = pl.BlockSpec(memory_space=pl.ANY)


def placed_out(out):
    return FAST if isinstance(out, jax.ShapeDtypeStruct) else SLOW


def local_call(kernel, out_shape, specs, name, flops, scratch=(), after=()):
    count = len(specs)

    def body(*refs):
        kernel(*refs[:count], *refs[count + len(after) :])

    call = pl.pallas_call(
        body,
        out_shape=out_shape,
        in_specs=list(specs) + [ANY] * len(after),
        out_specs=jax.tree.map(placed_out, out_shape),
        scratch_shapes=list(scratch),
        compiler_params=pltpu.CompilerParams(vmem_limit_bytes=VMEM),
        cost_estimate=pl.CostEstimate(flops=flops, bytes_accessed=2_000_000, transcendentals=0),
        name=name,
    )

    def placed(operand, spec):
        return pltpu.with_memory_space_constraint(operand, pltpu.HBM) if spec is SLOW else operand

    return lambda *operands: call(*map(placed, operands, specs), *after)


def gate(value, *after):
    return pl.pallas_call(
        lambda *refs: None,
        out_shape=jax.ShapeDtypeStruct(value.shape, value.dtype),
        in_specs=[ANY] * (1 + len(after)),
        out_specs=ANY,
        input_output_aliases={0: 0},
        name="gate",
    )(value, *after)


def started(sems, pairs):
    copies = [pltpu.make_async_copy(a, b, sems.at[i]) for i, (a, b) in enumerate(pairs)]
    for copy in copies:
        copy.start()
    return copies


def finished(copies):
    for copy in copies:
        copy.wait()


def fill_ext(x, halo_ref, ext, streams):
    for slot, stream in enumerate(streams):
        ext[slot, 6:8] = halo_ref[stream]
        for lo in range(0, x.shape[1], 32):
            ext[slot, lo + 8 : lo + 40] = x[slot, lo : lo + 32].astype(jnp.float32)


def featured_rows(ext, taps_ref, slot, stream, lo, rows):
    taps = taps_ref[stream]
    total = taps[0:1] * ext[slot, lo + 8 : lo + 8 + rows]
    for j in (1, 2):
        total += taps[j : j + 1] * ext[slot, lo + 8 - j : lo + 8 - j + rows]
    return total


def ends_kernel(
    feats, halo_ref, taps_hbm, decay_hbm, out_ref, prod_hbm, gate_hbm,
    x, taps, rate, prod, gate_rows, ext, sems, out_sems,
):
    finished(started(sems, ((feats, x), (taps_hbm, taps), (decay_hbm, rate))))
    rows, order = x.shape[1], rate.shape[0]
    fill_ext(x, halo_ref, ext, (0, 1, 2))
    for lo in range(0, rows, 16):
        gate_rows[lo : lo + 16] = featured_rows(ext, taps, 0, 0, lo, 16)
        first = featured_rows(ext, taps, 1, 1, lo, 16)
        prod[lo : lo + 16] = first * featured_rows(ext, taps, 2, 2, lo, 16)
    written = started(out_sems, ((prod, prod_hbm), (gate_rows, gate_hbm)))
    decay = jnp.exp(-rate[...])

    def body(i, state):
        block = prod[pl.ds(pl.multiple_of(i * 8, 8), 8), :]
        for j in range(8):
            state = decay * state + block[j : j + 1]
        return state

    state = lax.fori_loop(0, rows // 8, body, jnp.zeros(rate.shape, jnp.float32))
    for j in range(state.shape[1] // HEAD):
        block = state[:, j * HEAD : (j + 1) * HEAD]
        high = block.astype(jnp.bfloat16)
        out_ref[0, j * order : (j + 1) * order] = high
        out_ref[1, j * order : (j + 1) * order] = (block - high.astype(jnp.float32)).astype(
            jnp.bfloat16
        )
    finished(written)


def combine_kernel(place_ref, rate_hbm, own_ref, other_ref, out_ref, rate_ref, ends, sems):
    finished(started(sems, ((rate_hbm, rate_ref),)))
    x, z, k = place_ref[0], place_ref[1], place_ref[2]
    rate = rate_ref[...]
    order = rate.shape[0]

    def over(blocks):
        return jnp.exp(rate * (-128.0 * jnp.maximum(blocks, 0).astype(jnp.float32)))

    for row in range(NX):
        for side, ref in enumerate((own_ref, other_ref)):
            both = ref[row, 2 * NZ].astype(jnp.float32) + ref[row, 2 * NZ + 1].astype(jnp.float32)
            for j in range(rate.shape[1] // HEAD):
                lanes = slice(j * HEAD, (j + 1) * HEAD)
                ends[row, side, :, lanes] = both[j * order : (j + 1) * order]

    def end_of(row, core):
        return ends[row, jnp.where(k == core, 0, 1)]

    step, across, rest = over(jnp.int32(1)), over(jnp.int32(NZ * NK)), over(NZ * NK - NK * z - NK)
    earlier = jnp.zeros(rate.shape, jnp.float32)
    for row in range(NX - 1):
        whole = rest * (step * end_of(row, 0) + end_of(row, 1))
        earlier = jnp.where(x > row, across * earlier + whole, earlier)
    for target in range(NZ):
        total = over(NK * target + k) * earlier
        for core in range(NK):
            blocks = (NK * target + k) - (NK * z + core) - 1
            total = total + jnp.where(blocks >= 0, over(blocks) * end_of(x, core), 0.0)
        out_ref[target] = total


def one_less_exp(y):
    series = 1.0 - y / 9.0
    for n in range(8, 1, -1):
        series = 1.0 - y / n * series
    return jnp.where(y < 0.5, y * series, 1.0 - jnp.exp(-y))


def mix_kernel(
    rate_hbm, residue_hbm, parts_ref, prod_hbm, gate_hbm, out_ref,
    rate, residue, prod, gate_rows, sems,
):
    pairs = ((rate_hbm, rate), (residue_hbm, residue), (prod_hbm, prod), (gate_hbm, gate_rows))
    finished(started(sems, pairs))
    rows, width = prod.shape
    decay = jnp.exp(-rate[...])
    start = parts_ref[0]
    for z in range(1, NZ):
        start = start + parts_ref[z]
    rho = residue[...] * jnp.sqrt(one_less_exp(2.0 * rate[...]) / rate.shape[0])
    sub = lax.broadcasted_iota(jnp.int32, (8, width), 0)

    def body(i, state):
        base = pl.multiple_of(i * 16, 16)
        mixed = []
        for half in range(2):
            block = prod[pl.ds(base + 8 * half, 8), :]
            conv = jnp.zeros((8, width), jnp.float32)
            for j in range(8):
                state = decay * state + block[j : j + 1]
                row = jnp.sum(rho * state, axis=0, keepdims=True)
                conv = jnp.where(sub == j, row, conv)
            mixed.append(conv * gate_rows[pl.ds(base + 8 * half, 8), :])
        out_ref[pl.ds(base, 16), :] = jnp.concatenate(mixed, axis=0).astype(jnp.bfloat16)
        return state

    lax.fori_loop(0, rows // 16, body, start)


def pack_kernel(qkv, feats, out_ref, halo_ref, tail, sems):
    rows = qkv.shape[1]
    lanes = [pl.ds(head * HEAD, HEAD) for head in range(NZ)]
    pairs = [(qkv.at[:, :, lanes[i]], out_ref.at[i]) for i in range(NZ)]
    pairs.append((feats.at[:, pl.ds(rows - 16, 16), :], tail))
    finished(started(sems, pairs))
    halo_ref[...] = tail[...].astype(jnp.float32)[:, 14:16]


def halves_kernel(place_ref, weight_ref, same_ref, other_ref):
    for half in range(NZ0):

        @pl.when(place_ref[0] % NZ0 == half)
        def _():
            for ref, z0 in ((same_ref, half), (other_ref, 1 - half)):
                for part in range(NZ1):
                    lo = (2 * part + z0) * HEAD
                    ref[part] = weight_ref[lo : lo + HEAD]


def stack_kernel(place_ref, r0, r1, r2, r3, out, sems):
    pairs = [
        (ref, out.at[(place_ref[0] + NZ - steps) % NZ]) for steps, ref in enumerate((r0, r1, r2, r3))
    ]
    finished(started(sems, pairs))


def spread_kernel(qkv_ref, ends_ref, out, sems):
    pairs = []
    for i in range(NX):
        pairs += [
            (qkv_ref.at[z, pl.ds(1, 2)], out.at[i, pl.ds(2 * z, 2)]) for z in range(NZ)
        ] + [(ends_ref, out.at[i, pl.ds(2 * NZ, 2)])]
    finished(started(sems, pairs))


def folded(q, pairs, top, total, acc, visible=None):
    keys = pairs[:, 0].reshape(-1, HEAD)
    values = pairs[:, 1].reshape(-1, HEAD)
    s = lax.dot_general(keys, q, (((1,), (1,)), ((), ())), preferred_element_type=jnp.float32)
    if visible is not None:
        s = jnp.where(visible, s, -1e30)
    new = jnp.maximum(top, jnp.max(s, axis=0, keepdims=True))
    p = jnp.exp2((s - new) * SCALE)
    again = jnp.exp2((top - new) * SCALE)
    added = jnp.dot(values.T, p.astype(jnp.bfloat16), preferred_element_type=jnp.float32)
    return new, total * again + jnp.sum(p, axis=0, keepdims=True), acc * again + added


def pairs_of(ref, row):
    return ref[row, 0 : 2 * NZ].reshape(NZ, 2, HEAD, HEAD)


def fold_rows(x, q, ref, top, total, acc):
    for row in range(NX - 1):

        @pl.when(x > row)
        def _():
            top[...], total[...], acc[...] = folded(
                q, pairs_of(ref, row), top[...], total[...], acc[...]
            )


def own_kernel(place_ref, qkv_ref, kv_ref, top_ref, total_ref, acc_ref):
    x = place_ref[0]
    rows = NZ * HEAD
    q = qkv_ref[:, 0].reshape(rows, HEAD)
    col = lax.broadcasted_iota(jnp.int32, (1, rows), 1)
    row = lax.broadcasted_iota(jnp.int32, (rows, 1), 0)
    lowest = jnp.full((1, rows), -1e30, jnp.float32)
    nothing = jnp.zeros((1, rows), jnp.float32), jnp.zeros((HEAD, rows), jnp.float32)
    top_ref[...], total_ref[...], acc_ref[...] = folded(
        q, pairs_of(kv_ref, x), lowest, *nothing, row <= col
    )
    fold_rows(x, q, kv_ref, top_ref, total_ref, acc_ref)


def other_kernel(
    place_ref, qkv_ref, top_ref, total_ref, acc_ref, kv_ref, out_ref, top, total, acc
):
    x, k = place_ref[0], place_ref[1]
    rows = NZ * HEAD
    q = qkv_ref[:, 0].reshape(rows, HEAD)
    col = lax.broadcasted_iota(jnp.int32, (1, rows), 1)
    row = lax.broadcasted_iota(jnp.int32, (rows, 1), 0)
    here = (2 * (col // HEAD) + k) * HEAD + col % HEAD
    there = (2 * (row // HEAD) + 1 - k) * HEAD + row % HEAD
    top[...], total[...], acc[...] = folded(
        q, pairs_of(kv_ref, x), top_ref[...], total_ref[...], acc_ref[...], there <= here
    )
    fold_rows(x, q, kv_ref, top, total, acc)
    result = (acc[...] / total[...]).T.astype(jnp.bfloat16).reshape(out_ref.shape[1:])
    for h in range(NH):
        out_ref[h] = result


def project_kernel(place_ref, g0, g1, g2, g3, w_hbm, mine_ref, other_ref, held, parts, acc, sems):
    y, z0 = place_ref[0], place_ref[1]
    copies = started(sems, [(w_hbm.at[i], parts.at[i]) for i in range(NX)])
    for step, group in zip((0, 1, 3, 2), (g0, g1, g2, g3)):
        held[step] = group[...]
    for i in range(0, NX, 2):
        steps = [(2 * y - i - n + NX) % NX for n in range(2)]
        heads = jnp.concatenate([held[n, j] for n in steps for j in range(NH * NZ1)], axis=1)
        finished(copies[i : i + 2])
        for k in range(NK):
            for b in range(2):
                columns = [
                    parts[i + n, k, 2 * h + b].reshape(2 * HEAD, 256)
                    for n in range(2)
                    for h in range(NH)
                ]
                term = jnp.dot(
                    heads, jnp.concatenate(columns, axis=0), preferred_element_type=jnp.float32
                )
                lanes = slice(b * 256, b * 256 + 256)
                if i == 0:
                    acc[k, :, lanes] = term
                else:
                    acc[k, :, lanes] += term
    rows = mine_ref.shape[0]
    near_rows = pl.ds(pl.multiple_of(z0 * rows, rows), rows)
    far_rows = pl.ds(pl.multiple_of((1 - z0) * rows, rows), rows)
    for b in range(2):
        for k in range(NK):
            lo = (2 * b + k) * 256
            lanes = slice(b * 256, b * 256 + 256)
            mine_ref[:, lo : lo + 256] = acc[k, near_rows, lanes]
            other_ref[:, lo : lo + 256] = acc[k, far_rows, lanes].astype(jnp.bfloat16)


def per_device(hyena_feats, short_taps, decay_rate, residue, attn_qkv, out_weight):
    rows, width = hyena_feats.shape[1:]
    x, k, y = lax.axis_index("x"), lax.axis_index("k"), lax.axis_index("y")
    z1, z0 = lax.axis_index("z1"), lax.axis_index("z0")
    swap = [(0, 1), (1, 0)]
    short = jax.ShapeDtypeStruct
    bf16, f32 = jnp.bfloat16, jnp.float32
    dma = pltpu.SemaphoreType.DMA

    packed, tail = local_call(
        pack_kernel,
        (short((NZ, 3, rows, HEAD), bf16), short((3, 2, width), f32)),
        (SLOW, SLOW),
        "pack",
        10**8,
        (pltpu.VMEM((3, 16, width), bf16), dma((1 + NZ,))),
    )(attn_qkv, hyena_feats)
    qkv = lax.all_to_all(packed, ("z1", "z0"), 0, 0)
    halo = lax.ppermute(tail, ALL, moved(next_ctx))
    plane = short((rows, width), f32)
    poles = short(decay_rate.shape, f32)
    ends, prod, gate_rows = local_call(
        ends_kernel,
        (
            short((2, rows, HEAD), bf16),
            pltpu.HBM(plane.shape, f32),
            pltpu.HBM(plane.shape, f32),
        ),
        (SLOW, FAST, SLOW, SLOW),
        "ends",
        10**9,
        (
            pltpu.VMEM((3, rows, width), bf16),
            pltpu.VMEM(short_taps.shape, f32),
            pltpu.VMEM(poles.shape, f32),
            pltpu.VMEM(plane.shape, f32),
            pltpu.VMEM(plane.shape, f32),
            pltpu.VMEM((3, rows + 8, width), f32),
            dma((3,)),
            dma((2,)),
        ),
    )(hyena_feats, halo, short_taps, decay_rate)
    moved_weight = lax.ppermute(out_weight, ALL, moved(place_weight))
    spread = local_call(
        spread_kernel,
        pltpu.HBM((NX, 2 * NZ + 2, rows, HEAD), bf16),
        (FAST, FAST),
        "spread",
        10**8,
        (dma((NX * (NZ + 1),)),),
        after=(moved_weight,),
    )(qkv, ends)
    far_own = lax.all_to_all(spread, "x", 0, 0)
    far_other = lax.ppermute(far_own, "k", swap)

    z = (2 * z1 + z0).reshape(1)
    half = short((NZ1, HEAD, out_weight.shape[1]), bf16)
    same, opposite = local_call(
        halves_kernel, (half, half), (SMEM, FAST), "halves", 10**8, after=(spread,)
    )(z, moved_weight)
    arrived = [same] + [
        lax.ppermute(opposite if steps % 2 else same, ALL, along_z(steps)) for steps in (1, 2, 3)
    ]
    placed = local_call(
        stack_kernel, pltpu.HBM((NZ, *half.shape), bf16), (SMEM,) + (FAST,) * NZ, "stack", 10**8,
        (dma((NZ,)),),
        after=(far_own,),
    )(z, *arrived)
    weight = lax.all_gather(placed, ("x", "k")).reshape(NX, NK, *placed.shape)

    where = jnp.stack([x, k])
    line = short((1, NZ * rows), f32)
    square = short((HEAD, NZ * rows), f32)
    partial = local_call(
        own_kernel, (line, line, square), (SMEM, FAST, FAST), "own", 2 * 10**9
    )(where, qkv, far_own)
    attended = local_call(
        other_kernel,
        short((NH, NZ1, NZ0 * rows, HEAD), bf16),
        (SMEM,) + (FAST,) * 5,
        "other",
        2 * 10**9,
        [pltpu.VMEM(part.shape, f32) for part in (line, line, square)],
    )(where, qkv, *partial, far_other)
    group = lax.all_to_all(attended.reshape(NH * NZ1, NZ0 * rows, HEAD), ("h", "z1"), 0, 0)
    groups = [group] + [
        lax.ppermute(group, "y", [(i, (i + step) % NY) for i in range(NY)]) for step in (1, 3, 2)
    ]

    parts = local_call(
        combine_kernel,
        short((NZ, *poles.shape), f32),
        (SMEM, SLOW, FAST, FAST),
        "combine",
        10**8,
        (pltpu.VMEM(poles.shape, f32), pltpu.VMEM((NX, NK, *poles.shape), f32), dma((1,))),
        after=(group,),
    )(jnp.stack([x, 2 * z1 + z0, k]), decay_rate, far_own, far_other)
    parts = lax.all_to_all(parts, ("z1", "z0"), 0, 0)

    mine, other = local_call(
        project_kernel,
        (short((rows, width), f32), short((rows, width), bf16)),
        (SMEM,) + (FAST,) * 4 + (SLOW,),
        "project",
        2 * 10**9,
        (
            pltpu.VMEM((NY, *group.shape), bf16),
            pltpu.VMEM(weight.shape, bf16),
            pltpu.VMEM((NK, NZ0 * rows, width // 2), f32),
            dma((NX,)),
        ),
    )(jnp.stack([y, z0]), *groups, weight)
    received = lax.ppermute(other, "z0", swap)

    hyena_mixed = local_call(
        mix_kernel,
        short((rows, width), bf16),
        (SLOW, SLOW, FAST, SLOW, SLOW),
        "mix",
        4 * 10**9,
        (
            pltpu.VMEM(poles.shape, f32),
            pltpu.VMEM(poles.shape, f32),
            pltpu.VMEM(plane.shape, f32),
            pltpu.VMEM(plane.shape, f32),
            dma((4,)),
        ),
    )(decay_rate, residue, parts, prod, gate_rows)
    return hyena_mixed, (mine + received.astype(f32)).astype(bf16)


def solution(mesh):
    fine = Mesh(mesh.devices.reshape(NX, NZ1, NZ0, NK, NY, NH), ALL)
    ctx, tp = ("x", "z1", "z0", "k"), ("y", "h")
    return jax.shard_map(
        per_device,
        mesh=fine,
        in_specs=(
            P(None, ctx, tp),
            P(None, None, tp),
            P(None, tp),
            P(None, tp),
            P(None, ctx, tp),
            P(tp, ctx),
        ),
        out_specs=(P(ctx, tp), P(ctx, tp)),
        check_vma=False,
    )
```

```python
import math

import jax
import jax.numpy as jnp
from jax import lax
from jax.experimental import pallas as pl
from jax.experimental.pallas import tpu as pltpu
from jax.sharding import Mesh, PartitionSpec as P

HEAD = 128
NX, NZ1, NZ0, NK, NY, NH = 4, 2, 2, 2, 4, 2
NZ = NZ1 * NZ0
ALL = ("x", "z1", "z0", "k", "y", "h")
SIZES = dict(x=NX, z1=NZ1, z0=NZ0, k=NK, y=NY, h=NH)
SCALE = math.log2(math.e) / math.sqrt(HEAD)
VMEM = 48 * 1024 * 1024


def linear(**c):
    index = 0
    for name in ALL:
        index = index * SIZES[name] + c[name]
    return index


def places():
    for index in range(256):
        rest, c = index, {}
        for name in reversed(ALL):
            c[name] = rest % SIZES[name]
            rest //= SIZES[name]
        yield c


def moved(change):
    pairs = []
    for c in places():
        d = change(**c)
        if d is not None:
            pairs.append((linear(**c), linear(**dict(c, **d))))
    return pairs


def next_ctx(x, z1, z0, k, **_):
    place = ((x * NZ1 + z1) * NZ0 + z0) * NK + k + 1
    if place == NX * NZ * NK:
        return None
    return dict(x=place // (NZ * NK), z1=place // 4 % 2, z0=place // 2 % 2, k=place % 2)


def along_z(steps):
    def change(z1, z0, **_):
        z = (2 * z1 + z0 + steps) % NZ
        return dict(z1=z // 2, z0=z % 2)

    return moved(change)


def place_weight(x, z1, z0, k, y, h):
    return dict(x=(x + y) % NX, z1=h, z0=z0, k=k, y=x, h=z1)


SMEM = pl.BlockSpec(memory_space=pltpu.SMEM)
FAST = pl.BlockSpec(memory_space=pltpu.VMEM)
SLOW = pl.BlockSpec(memory_space=pltpu.HBM)
ANY = pl.BlockSpec(memory_space=pl.ANY)


def placed_out(out):
    return FAST if isinstance(out, jax.ShapeDtypeStruct) else SLOW


def local_call(kernel, out_shape, specs, name, flops, scratch=(), after=()):
    count = len(specs)

    def body(*refs):
        kernel(*refs[:count], *refs[count + len(after) :])

    call = pl.pallas_call(
        body,
        out_shape=out_shape,
        in_specs=list(specs) + [ANY] * len(after),
        out_specs=jax.tree.map(placed_out, out_shape),
        scratch_shapes=list(scratch),
        compiler_params=pltpu.CompilerParams(vmem_limit_bytes=VMEM),
        cost_estimate=pl.CostEstimate(flops=flops, bytes_accessed=2_000_000, transcendentals=0),
        name=name,
    )

    def placed(operand, spec):
        return pltpu.with_memory_space_constraint(operand, pltpu.HBM) if spec is SLOW else operand

    return lambda *operands: call(*map(placed, operands, specs), *after)


def gate(value, *after):
    return pl.pallas_call(
        lambda *refs: None,
        out_shape=jax.ShapeDtypeStruct(value.shape, value.dtype),
        in_specs=[ANY] * (1 + len(after)),
        out_specs=ANY,
        input_output_aliases={0: 0},
        name="gate",
    )(value, *after)


def started(sems, pairs):
    copies = [pltpu.make_async_copy(a, b, sems.at[i]) for i, (a, b) in enumerate(pairs)]
    for copy in copies:
        copy.start()
    return copies


def finished(copies):
    for copy in copies:
        copy.wait()


def fill_ext(x, halo_ref, ext, streams):
    for slot, stream in enumerate(streams):
        ext[slot, 6:8] = halo_ref[stream]
        for lo in range(0, x.shape[1], 32):
            ext[slot, lo + 8 : lo + 40] = x[slot, lo : lo + 32].astype(jnp.float32)


def featured_rows(ext, taps_ref, slot, stream, lo, rows):
    taps = taps_ref[stream]
    total = taps[0:1] * ext[slot, lo + 8 : lo + 8 + rows]
    for j in (1, 2):
        total += taps[j : j + 1] * ext[slot, lo + 8 - j : lo + 8 - j + rows]
    return total


def ends_kernel(
    feats, halo_ref, taps_hbm, decay_hbm, out_ref, prod_hbm, gate_hbm,
    x, taps, rate, prod, gate_rows, ext, sems, out_sems,
):
    finished(started(sems, ((feats, x), (taps_hbm, taps), (decay_hbm, rate))))
    rows, order = x.shape[1], rate.shape[0]
    fill_ext(x, halo_ref, ext, (0, 1, 2))
    for lo in range(0, rows, 16):
        gate_rows[lo : lo + 16] = featured_rows(ext, taps, 0, 0, lo, 16)
        first = featured_rows(ext, taps, 1, 1, lo, 16)
        prod[lo : lo + 16] = first * featured_rows(ext, taps, 2, 2, lo, 16)
    written = started(out_sems, ((prod, prod_hbm), (gate_rows, gate_hbm)))
    decay = jnp.exp(-rate[...])

    def body(i, state):
        block = prod[pl.ds(pl.multiple_of(i * 8, 8), 8), :]
        for j in range(8):
            state = decay * state + block[j : j + 1]
        return state

    state = lax.fori_loop(0, rows // 8, body, jnp.zeros(rate.shape, jnp.float32))
    for j in range(state.shape[1] // HEAD):
        block = state[:, j * HEAD : (j + 1) * HEAD]
        high = block.astype(jnp.bfloat16)
        out_ref[0, j * order : (j + 1) * order] = high
        out_ref[1, j * order : (j + 1) * order] = (block - high.astype(jnp.float32)).astype(
            jnp.bfloat16
        )
    finished(written)


def combine_kernel(place_ref, rate_hbm, own_ref, other_ref, out_ref, rate_ref, ends, sems):
    finished(started(sems, ((rate_hbm, rate_ref),)))
    x, z, k = place_ref[0], place_ref[1], place_ref[2]
    rate = rate_ref[...]
    order = rate.shape[0]

    def over(blocks):
        return jnp.exp(rate * (-128.0 * jnp.maximum(blocks, 0).astype(jnp.float32)))

    for row in range(NX):
        for side, ref in enumerate((own_ref, other_ref)):
            both = ref[row, 2 * NZ].astype(jnp.float32) + ref[row, 2 * NZ + 1].astype(jnp.float32)
            for j in range(rate.shape[1] // HEAD):
                lanes = slice(j * HEAD, (j + 1) * HEAD)
                ends[row, side, :, lanes] = both[j * order : (j + 1) * order]

    def end_of(row, core):
        return ends[row, jnp.where(k == core, 0, 1)]

    step, across, rest = over(jnp.int32(1)), over(jnp.int32(NZ * NK)), over(NZ * NK - NK * z - NK)
    earlier = jnp.zeros(rate.shape, jnp.float32)
    for row in range(NX - 1):
        whole = rest * (step * end_of(row, 0) + end_of(row, 1))
        earlier = jnp.where(x > row, across * earlier + whole, earlier)
    for target in range(NZ):
        total = over(NK * target + k) * earlier
        for core in range(NK):
            blocks = (NK * target + k) - (NK * z + core) - 1
            total = total + jnp.where(blocks >= 0, over(blocks) * end_of(x, core), 0.0)
        out_ref[target] = total


def one_less_exp(y):
    series = 1.0 - y / 9.0
    for n in range(8, 1, -1):
        series = 1.0 - y / n * series
    return jnp.where(y < 0.5, y * series, 1.0 - jnp.exp(-y))


def mix_kernel(
    rate_hbm, residue_hbm, parts_ref, prod_hbm, gate_hbm, out_ref,
    rate, residue, prod, gate_rows, sems,
):
    pairs = ((rate_hbm, rate), (residue_hbm, residue), (prod_hbm, prod), (gate_hbm, gate_rows))
    finished(started(sems, pairs))
    rows, width = prod.shape
    decay = jnp.exp(-rate[...])
    start = parts_ref[0]
    for z in range(1, NZ):
        start = start + parts_ref[z]
    rho = residue[...] * jnp.sqrt(one_less_exp(2.0 * rate[...]) / rate.shape[0])
    sub = lax.broadcasted_iota(jnp.int32, (8, width), 0)

    def body(i, state):
        base = pl.multiple_of(i * 16, 16)
        mixed = []
        for half in range(2):
            block = prod[pl.ds(base + 8 * half, 8), :]
            conv = jnp.zeros((8, width), jnp.float32)
            for j in range(8):
                state = decay * state + block[j : j + 1]
                row = jnp.sum(rho * state, axis=0, keepdims=True)
                conv = jnp.where(sub == j, row, conv)
            mixed.append(conv * gate_rows[pl.ds(base + 8 * half, 8), :])
        out_ref[pl.ds(base, 16), :] = jnp.concatenate(mixed, axis=0).astype(jnp.bfloat16)
        return state

    lax.fori_loop(0, rows // 16, body, start)


def pack_kernel(qkv, feats, out_ref, halo_ref, tail, sems):
    rows = qkv.shape[1]
    lanes = [pl.ds(head * HEAD, HEAD) for head in range(NZ)]
    pairs = [(qkv.at[:, :, lanes[i]], out_ref.at[i]) for i in range(NZ)]
    pairs.append((feats.at[:, pl.ds(rows - 16, 16), :], tail))
    finished(started(sems, pairs))
    halo_ref[...] = tail[...].astype(jnp.float32)[:, 14:16]


def halves_kernel(place_ref, weight_ref, same_ref, other_ref):
    for half in range(NZ0):

        @pl.when(place_ref[0] % NZ0 == half)
        def _():
            for ref, z0 in ((same_ref, half), (other_ref, 1 - half)):
                for part in range(NZ1):
                    lo = (2 * part + z0) * HEAD
                    ref[part] = weight_ref[lo : lo + HEAD]


def stack_kernel(place_ref, *refs):
    for steps, ref in enumerate(refs[:-1]):
        refs[-1][(place_ref[0] + NZ - steps) % NZ] = ref[...]


def spread_kernel(qkv_ref, ends_ref, out_ref):
    for z in range(NZ):
        for i in range(out_ref.shape[0]):
            out_ref[i, 2 * z : 2 * z + 2] = qkv_ref[z, 1:]
    for i in range(out_ref.shape[0]):
        out_ref[i, 2 * NZ :] = ends_ref[...]


def folded(q, pairs, top, total, acc, visible=None):
    keys = pairs[:, 0].reshape(-1, HEAD)
    values = pairs[:, 1].reshape(-1, HEAD)
    s = lax.dot_general(keys, q, (((1,), (1,)), ((), ())), preferred_element_type=jnp.float32)
    if visible is not None:
        s = jnp.where(visible, s, -1e30)
    new = jnp.maximum(top, jnp.max(s, axis=0, keepdims=True))
    p = jnp.exp2((s - new) * SCALE)
    again = jnp.exp2((top - new) * SCALE)
    added = jnp.dot(values.T, p.astype(jnp.bfloat16), preferred_element_type=jnp.float32)
    return new, total * again + jnp.sum(p, axis=0, keepdims=True), acc * again + added


def pairs_of(ref, row):
    return ref[row, 0 : 2 * NZ].reshape(NZ, 2, HEAD, HEAD)


def fold_rows(x, q, ref, top, total, acc):
    for row in range(NX - 1):

        @pl.when(x > row)
        def _():
            top[...], total[...], acc[...] = folded(
                q, pairs_of(ref, row), top[...], total[...], acc[...]
            )


def own_kernel(place_ref, qkv_ref, kv_ref, top_ref, total_ref, acc_ref):
    x = place_ref[0]
    rows = NZ * HEAD
    q = qkv_ref[:, 0].reshape(rows, HEAD)
    col = lax.broadcasted_iota(jnp.int32, (1, rows), 1)
    row = lax.broadcasted_iota(jnp.int32, (rows, 1), 0)
    lowest = jnp.full((1, rows), -1e30, jnp.float32)
    nothing = jnp.zeros((1, rows), jnp.float32), jnp.zeros((HEAD, rows), jnp.float32)
    top_ref[...], total_ref[...], acc_ref[...] = folded(
        q, pairs_of(kv_ref, x), lowest, *nothing, row <= col
    )
    fold_rows(x, q, kv_ref, top_ref, total_ref, acc_ref)


def other_kernel(
    place_ref, qkv_ref, top_ref, total_ref, acc_ref, kv_ref, out_ref, top, total, acc
):
    x, k = place_ref[0], place_ref[1]
    rows = NZ * HEAD
    q = qkv_ref[:, 0].reshape(rows, HEAD)
    col = lax.broadcasted_iota(jnp.int32, (1, rows), 1)
    row = lax.broadcasted_iota(jnp.int32, (rows, 1), 0)
    here = (2 * (col // HEAD) + k) * HEAD + col % HEAD
    there = (2 * (row // HEAD) + 1 - k) * HEAD + row % HEAD
    top[...], total[...], acc[...] = folded(
        q, pairs_of(kv_ref, x), top_ref[...], total_ref[...], acc_ref[...], there <= here
    )
    fold_rows(x, q, kv_ref, top, total, acc)
    result = (acc[...] / total[...]).T.astype(jnp.bfloat16).reshape(out_ref.shape[1:])
    for h in range(NH):
        out_ref[h] = result


def project_kernel(place_ref, g0, g1, g2, g3, w_hbm, mine_ref, other_ref, held, parts, acc, sems):
    y, z0 = place_ref[0], place_ref[1]
    copies = started(sems, [(w_hbm.at[i], parts.at[i]) for i in range(NX)])
    for step, group in zip((0, 1, 3, 2), (g0, g1, g2, g3)):
        held[step] = group[...]
    for i in range(NX):
        step = (2 * y - i + NX) % NX
        heads = jnp.concatenate([held[step, j] for j in range(NH * NZ1)], axis=1)
        copies[i].wait()
        for k in range(NK):
            for b in range(2):
                columns = [parts[i, k, 2 * h + b].reshape(2 * HEAD, 256) for h in range(NH)]
                term = jnp.dot(
                    heads, jnp.concatenate(columns, axis=0), preferred_element_type=jnp.float32
                )
                lanes = slice(b * 256, b * 256 + 256)
                if i == 0:
                    acc[k, :, lanes] = term
                else:
                    acc[k, :, lanes] += term
    rows = mine_ref.shape[0]
    near_rows = pl.ds(pl.multiple_of(z0 * rows, rows), rows)
    far_rows = pl.ds(pl.multiple_of((1 - z0) * rows, rows), rows)
    for b in range(2):
        for k in range(NK):
            lo = (2 * b + k) * 256
            lanes = slice(b * 256, b * 256 + 256)
            mine_ref[:, lo : lo + 256] = acc[k, near_rows, lanes]
            other_ref[:, lo : lo + 256] = acc[k, far_rows, lanes].astype(jnp.bfloat16)


def per_device(hyena_feats, short_taps, decay_rate, residue, attn_qkv, out_weight):
    rows, width = hyena_feats.shape[1:]
    x, k, y = lax.axis_index("x"), lax.axis_index("k"), lax.axis_index("y")
    z1, z0 = lax.axis_index("z1"), lax.axis_index("z0")
    swap = [(0, 1), (1, 0)]
    short = jax.ShapeDtypeStruct
    bf16, f32 = jnp.bfloat16, jnp.float32
    dma = pltpu.SemaphoreType.DMA

    packed, tail = local_call(
        pack_kernel,
        (short((NZ, 3, rows, HEAD), bf16), short((3, 2, width), f32)),
        (SLOW, SLOW),
        "pack",
        10**8,
        (pltpu.VMEM((3, 16, width), bf16), dma((1 + NZ,))),
    )(attn_qkv, hyena_feats)
    qkv = lax.all_to_all(packed, ("z1", "z0"), 0, 0)
    halo = lax.ppermute(tail, ALL, moved(next_ctx))
    plane = short((rows, width), f32)
    poles = short(decay_rate.shape, f32)
    ends, prod, gate_rows = local_call(
        ends_kernel,
        (
            short((2, rows, HEAD), bf16),
            pltpu.HBM(plane.shape, f32),
            pltpu.HBM(plane.shape, f32),
        ),
        (SLOW, FAST, SLOW, SLOW),
        "ends",
        10**9,
        (
            pltpu.VMEM((3, rows, width), bf16),
            pltpu.VMEM(short_taps.shape, f32),
            pltpu.VMEM(poles.shape, f32),
            pltpu.VMEM(plane.shape, f32),
            pltpu.VMEM(plane.shape, f32),
            pltpu.VMEM((3, rows + 8, width), f32),
            dma((3,)),
            dma((2,)),
        ),
    )(hyena_feats, halo, short_taps, decay_rate)
    moved_weight = lax.ppermute(out_weight, ALL, moved(place_weight))
    spread = local_call(
        spread_kernel,
        short((NX, 2 * NZ + 2, rows, HEAD), bf16),
        (FAST, FAST),
        "spread",
        10**8,
        after=(moved_weight,),
    )(qkv, ends)
    far_own = lax.all_to_all(spread, "x", 0, 0)
    far_other = lax.ppermute(far_own, "k", swap)

    z = (2 * z1 + z0).reshape(1)
    half = short((NZ1, HEAD, out_weight.shape[1]), bf16)
    same, opposite = local_call(
        halves_kernel, (half, half), (SMEM, FAST), "halves", 10**8, after=(spread,)
    )(z, moved_weight)
    arrived = [same] + [
        lax.ppermute(opposite if steps % 2 else same, ALL, along_z(steps)) for steps in (1, 2, 3)
    ]
    placed = local_call(
        stack_kernel, short((NZ, *half.shape), bf16), (SMEM,) + (FAST,) * NZ, "stack", 10**8,
        after=(far_own,),
    )(z, *arrived)
    weight = lax.all_gather(placed, ("x", "k")).reshape(NX, NK, *placed.shape)

    where = jnp.stack([x, k])
    line = short((1, NZ * rows), f32)
    square = short((HEAD, NZ * rows), f32)
    partial = local_call(
        own_kernel, (line, line, square), (SMEM, FAST, FAST), "own", 2 * 10**9
    )(where, qkv, far_own)
    attended = local_call(
        other_kernel,
        short((NH, NZ1, NZ0 * rows, HEAD), bf16),
        (SMEM,) + (FAST,) * 5,
        "other",
        2 * 10**9,
        [pltpu.VMEM(part.shape, f32) for part in (line, line, square)],
    )(where, qkv, *partial, far_other)
    group = lax.all_to_all(attended.reshape(NH * NZ1, NZ0 * rows, HEAD), ("h", "z1"), 0, 0)
    groups = [group] + [
        lax.ppermute(group, "y", [(i, (i + step) % NY) for i in range(NY)]) for step in (1, 3, 2)
    ]

    parts = local_call(
        combine_kernel,
        short((NZ, *poles.shape), f32),
        (SMEM, SLOW, FAST, FAST),
        "combine",
        10**8,
        (pltpu.VMEM(poles.shape, f32), pltpu.VMEM((NX, NK, *poles.shape), f32), dma((1,))),
        after=(group,),
    )(jnp.stack([x, 2 * z1 + z0, k]), decay_rate, far_own, far_other)
    parts = lax.all_to_all(parts, ("z1", "z0"), 0, 0)

    mine, other = local_call(
        project_kernel,
        (short((rows, width), f32), short((rows, width), bf16)),
        (SMEM,) + (FAST,) * 4 + (SLOW,),
        "project",
        2 * 10**9,
        (
            pltpu.VMEM((NY, *group.shape), bf16),
            pltpu.VMEM(weight.shape, bf16),
            pltpu.VMEM((NK, NZ0 * rows, width // 2), f32),
            dma((NX,)),
        ),
    )(jnp.stack([y, z0]), *groups, weight)
    received = lax.ppermute(other, "z0", swap)

    hyena_mixed = local_call(
        mix_kernel,
        short((rows, width), bf16),
        (SLOW, SLOW, FAST, SLOW, SLOW),
        "mix",
        4 * 10**9,
        (
            pltpu.VMEM(poles.shape, f32),
            pltpu.VMEM(poles.shape, f32),
            pltpu.VMEM(plane.shape, f32),
            pltpu.VMEM(plane.shape, f32),
            dma((4,)),
        ),
    )(decay_rate, residue, parts, prod, gate_rows)
    return hyena_mixed, (mine + received.astype(f32)).astype(bf16)


def solution(mesh):
    fine = Mesh(mesh.devices.reshape(NX, NZ1, NZ0, NK, NY, NH), ALL)
    ctx, tp = ("x", "z1", "z0", "k"), ("y", "h")
    return jax.shard_map(
        per_device,
        mesh=fine,
        in_specs=(
            P(None, ctx, tp),
            P(None, None, tp),
            P(None, tp),
            P(None, tp),
            P(None, ctx, tp),
            P(tp, ctx),
        ),
        out_specs=(P(ctx, tp), P(ctx, tp)),
        check_vma=False,
    )
```

```python
import math

import jax
import jax.numpy as jnp
from jax import lax
from jax.experimental import pallas as pl
from jax.experimental.pallas import tpu as pltpu
from jax.sharding import Mesh, PartitionSpec as P

HEAD = 128
NX, NZ1, NZ0, NK, NY, NH = 4, 2, 2, 2, 4, 2
NZ = NZ1 * NZ0
ALL = ("x", "z1", "z0", "k", "y", "h")
SIZES = dict(x=NX, z1=NZ1, z0=NZ0, k=NK, y=NY, h=NH)
SCALE = math.log2(math.e) / math.sqrt(HEAD)
VMEM = 48 * 1024 * 1024


def linear(**c):
    index = 0
    for name in ALL:
        index = index * SIZES[name] + c[name]
    return index


def places():
    for index in range(256):
        rest, c = index, {}
        for name in reversed(ALL):
            c[name] = rest % SIZES[name]
            rest //= SIZES[name]
        yield c


def moved(change):
    pairs = []
    for c in places():
        d = change(**c)
        if d is not None:
            pairs.append((linear(**c), linear(**dict(c, **d))))
    return pairs


def next_ctx(x, z1, z0, k, **_):
    place = ((x * NZ1 + z1) * NZ0 + z0) * NK + k + 1
    if place == NX * NZ * NK:
        return None
    return dict(x=place // (NZ * NK), z1=place // 4 % 2, z0=place // 2 % 2, k=place % 2)


def along_z(steps):
    def change(z1, z0, **_):
        z = (2 * z1 + z0 + steps) % NZ
        return dict(z1=z // 2, z0=z % 2)

    return moved(change)


def place_weight(x, z1, z0, k, y, h):
    return dict(x=(x + y) % NX, z1=h, z0=z0, k=k, y=x, h=z1)


SMEM = pl.BlockSpec(memory_space=pltpu.SMEM)
FAST = pl.BlockSpec(memory_space=pltpu.VMEM)
SLOW = pl.BlockSpec(memory_space=pltpu.HBM)
ANY = pl.BlockSpec(memory_space=pl.ANY)


def placed_out(out):
    return FAST if isinstance(out, jax.ShapeDtypeStruct) else SLOW


def local_call(kernel, out_shape, specs, name, flops, scratch=(), after=()):
    count = len(specs)

    def body(*refs):
        kernel(*refs[:count], *refs[count + len(after) :])

    call = pl.pallas_call(
        body,
        out_shape=out_shape,
        in_specs=list(specs) + [ANY] * len(after),
        out_specs=jax.tree.map(placed_out, out_shape),
        scratch_shapes=list(scratch),
        compiler_params=pltpu.CompilerParams(vmem_limit_bytes=VMEM),
        cost_estimate=pl.CostEstimate(flops=flops, bytes_accessed=2_000_000, transcendentals=0),
        name=name,
    )

    def placed(operand, spec):
        return pltpu.with_memory_space_constraint(operand, pltpu.HBM) if spec is SLOW else operand

    return lambda *operands: call(*map(placed, operands, specs), *after)


def gate(value, *after):
    return pl.pallas_call(
        lambda *refs: None,
        out_shape=jax.ShapeDtypeStruct(value.shape, value.dtype),
        in_specs=[ANY] * (1 + len(after)),
        out_specs=ANY,
        input_output_aliases={0: 0},
        name="gate",
    )(value, *after)


def started(sems, pairs):
    copies = [pltpu.make_async_copy(a, b, sems.at[i]) for i, (a, b) in enumerate(pairs)]
    for copy in copies:
        copy.start()
    return copies


def finished(copies):
    for copy in copies:
        copy.wait()


def fill_ext(x, halo_ref, ext, streams):
    for slot, stream in enumerate(streams):
        ext[slot, 6:8] = halo_ref[stream]
        for lo in range(0, x.shape[1], 32):
            ext[slot, lo + 8 : lo + 40] = x[slot, lo : lo + 32].astype(jnp.float32)


def featured_rows(ext, taps_ref, slot, stream, lo, rows):
    taps = taps_ref[stream]
    total = taps[0:1] * ext[slot, lo + 8 : lo + 8 + rows]
    for j in (1, 2):
        total += taps[j : j + 1] * ext[slot, lo + 8 - j : lo + 8 - j + rows]
    return total


def ends_kernel(
    feats, halo_ref, taps_hbm, decay_hbm, out_ref, prod_hbm, gate_hbm,
    x, taps, rate, prod, gate_rows, ext, sems, out_sems,
):
    rows, order = x.shape[1], rate.shape[0]
    half = rows // 2
    pieces = [(i, pl.ds(lo, half)) for i in range(3) for lo in (0, half)]
    pairs = [(taps_hbm, taps), (decay_hbm, rate)]
    pairs += [(feats.at[i, part, :], x.at[i, part, :]) for i, part in pieces]
    finished(started(sems, pairs))
    fill_ext(x, halo_ref, ext, (0, 1, 2))
    for lo in range(0, rows, 16):
        gate_rows[lo : lo + 16] = featured_rows(ext, taps, 0, 0, lo, 16)
        first = featured_rows(ext, taps, 1, 1, lo, 16)
        prod[lo : lo + 16] = first * featured_rows(ext, taps, 2, 2, lo, 16)
    written = started(out_sems, ((prod, prod_hbm), (gate_rows, gate_hbm)))
    decay = jnp.exp(-rate[...])

    def body(i, state):
        block = prod[pl.ds(pl.multiple_of(i * 8, 8), 8), :]
        for j in range(8):
            state = decay * state + block[j : j + 1]
        return state

    state = lax.fori_loop(0, rows // 8, body, jnp.zeros(rate.shape, jnp.float32))
    for j in range(state.shape[1] // HEAD):
        block = state[:, j * HEAD : (j + 1) * HEAD]
        high = block.astype(jnp.bfloat16)
        out_ref[0, j * order : (j + 1) * order] = high
        out_ref[1, j * order : (j + 1) * order] = (block - high.astype(jnp.float32)).astype(
            jnp.bfloat16
        )
    finished(written)


def combine_kernel(place_ref, rate_hbm, own_ref, other_ref, out_ref, rate_ref, ends, sems):
    finished(started(sems, ((rate_hbm, rate_ref),)))
    x, z, k = place_ref[0], place_ref[1], place_ref[2]
    rate = rate_ref[...]
    order = rate.shape[0]

    def over(blocks):
        return jnp.exp(rate * (-128.0 * jnp.maximum(blocks, 0).astype(jnp.float32)))

    for row in range(NX):
        for side, ref in enumerate((own_ref, other_ref)):
            both = ref[row, 2 * NZ].astype(jnp.float32) + ref[row, 2 * NZ + 1].astype(jnp.float32)
            for j in range(rate.shape[1] // HEAD):
                lanes = slice(j * HEAD, (j + 1) * HEAD)
                ends[row, side, :, lanes] = both[j * order : (j + 1) * order]

    def end_of(row, core):
        return ends[row, jnp.where(k == core, 0, 1)]

    step, across, rest = over(jnp.int32(1)), over(jnp.int32(NZ * NK)), over(NZ * NK - NK * z - NK)
    earlier = jnp.zeros(rate.shape, jnp.float32)
    for row in range(NX - 1):
        whole = rest * (step * end_of(row, 0) + end_of(row, 1))
        earlier = jnp.where(x > row, across * earlier + whole, earlier)
    for target in range(NZ):
        total = over(NK * target + k) * earlier
        for core in range(NK):
            blocks = (NK * target + k) - (NK * z + core) - 1
            total = total + jnp.where(blocks >= 0, over(blocks) * end_of(x, core), 0.0)
        out_ref[target] = total


def one_less_exp(y):
    series = 1.0 - y / 9.0
    for n in range(8, 1, -1):
        series = 1.0 - y / n * series
    return jnp.where(y < 0.5, y * series, 1.0 - jnp.exp(-y))


def mix_kernel(
    rate_hbm, residue_hbm, parts_ref, prod_hbm, gate_hbm, out_ref,
    rate, residue, prod, gate_rows, sems,
):
    pairs = ((rate_hbm, rate), (residue_hbm, residue), (prod_hbm, prod), (gate_hbm, gate_rows))
    finished(started(sems, pairs))
    rows, width = prod.shape
    decay = jnp.exp(-rate[...])
    start = parts_ref[0]
    for z in range(1, NZ):
        start = start + parts_ref[z]
    rho = residue[...] * jnp.sqrt(one_less_exp(2.0 * rate[...]) / rate.shape[0])
    sub = lax.broadcasted_iota(jnp.int32, (8, width), 0)

    def body(i, state):
        base = pl.multiple_of(i * 16, 16)
        mixed = []
        for half in range(2):
            block = prod[pl.ds(base + 8 * half, 8), :]
            conv = jnp.zeros((8, width), jnp.float32)
            for j in range(8):
                state = decay * state + block[j : j + 1]
                row = jnp.sum(rho * state, axis=0, keepdims=True)
                conv = jnp.where(sub == j, row, conv)
            mixed.append(conv * gate_rows[pl.ds(base + 8 * half, 8), :])
        out_ref[pl.ds(base, 16), :] = jnp.concatenate(mixed, axis=0).astype(jnp.bfloat16)
        return state

    lax.fori_loop(0, rows // 16, body, start)


def pack_kernel(qkv, feats, out_ref, halo_ref, tail, sems):
    rows = qkv.shape[1]
    lanes = [pl.ds(head * HEAD, HEAD) for head in range(NZ)]
    pairs = [(qkv.at[:, :, lanes[i]], out_ref.at[i]) for i in range(NZ)]
    pairs.append((feats.at[:, pl.ds(rows - 16, 16), :], tail))
    finished(started(sems, pairs))
    halo_ref[...] = tail[...].astype(jnp.float32)[:, 14:16]


def halves_kernel(place_ref, weight_ref, same_ref, other_ref):
    for half in range(NZ0):

        @pl.when(place_ref[0] % NZ0 == half)
        def _():
            for ref, z0 in ((same_ref, half), (other_ref, 1 - half)):
                for part in range(NZ1):
                    lo = (2 * part + z0) * HEAD
                    ref[part] = weight_ref[lo : lo + HEAD]


def stack_kernel(place_ref, *refs):
    for steps, ref in enumerate(refs[:-1]):
        refs[-1][(place_ref[0] + NZ - steps) % NZ] = ref[...]


def spread_kernel(qkv_ref, ends_ref, out_ref):
    for z in range(NZ):
        for i in range(out_ref.shape[0]):
            out_ref[i, 2 * z : 2 * z + 2] = qkv_ref[z, 1:]
    for i in range(out_ref.shape[0]):
        out_ref[i, 2 * NZ :] = ends_ref[...]


def folded(q, pairs, top, total, acc, visible=None):
    keys = pairs[:, 0].reshape(-1, HEAD)
    values = pairs[:, 1].reshape(-1, HEAD)
    s = lax.dot_general(keys, q, (((1,), (1,)), ((), ())), preferred_element_type=jnp.float32)
    if visible is not None:
        s = jnp.where(visible, s, -1e30)
    new = jnp.maximum(top, jnp.max(s, axis=0, keepdims=True))
    p = jnp.exp2((s - new) * SCALE)
    again = jnp.exp2((top - new) * SCALE)
    added = jnp.dot(values.T, p.astype(jnp.bfloat16), preferred_element_type=jnp.float32)
    return new, total * again + jnp.sum(p, axis=0, keepdims=True), acc * again + added


def pairs_of(ref, row):
    return ref[row, 0 : 2 * NZ].reshape(NZ, 2, HEAD, HEAD)


def fold_rows(x, q, ref, top, total, acc):
    for row in range(NX - 1):

        @pl.when(x > row)
        def _():
            top[...], total[...], acc[...] = folded(
                q, pairs_of(ref, row), top[...], total[...], acc[...]
            )


def own_kernel(place_ref, qkv_ref, kv_ref, top_ref, total_ref, acc_ref):
    x = place_ref[0]
    rows = NZ * HEAD
    q = qkv_ref[:, 0].reshape(rows, HEAD)
    col = lax.broadcasted_iota(jnp.int32, (1, rows), 1)
    row = lax.broadcasted_iota(jnp.int32, (rows, 1), 0)
    lowest = jnp.full((1, rows), -1e30, jnp.float32)
    nothing = jnp.zeros((1, rows), jnp.float32), jnp.zeros((HEAD, rows), jnp.float32)
    top_ref[...], total_ref[...], acc_ref[...] = folded(
        q, pairs_of(kv_ref, x), lowest, *nothing, row <= col
    )
    fold_rows(x, q, kv_ref, top_ref, total_ref, acc_ref)


def other_kernel(
    place_ref, qkv_ref, top_ref, total_ref, acc_ref, kv_ref, out_ref, top, total, acc
):
    x, k = place_ref[0], place_ref[1]
    rows = NZ * HEAD
    q = qkv_ref[:, 0].reshape(rows, HEAD)
    col = lax.broadcasted_iota(jnp.int32, (1, rows), 1)
    row = lax.broadcasted_iota(jnp.int32, (rows, 1), 0)
    here = (2 * (col // HEAD) + k) * HEAD + col % HEAD
    there = (2 * (row // HEAD) + 1 - k) * HEAD + row % HEAD
    top[...], total[...], acc[...] = folded(
        q, pairs_of(kv_ref, x), top_ref[...], total_ref[...], acc_ref[...], there <= here
    )
    fold_rows(x, q, kv_ref, top, total, acc)
    result = (acc[...] / total[...]).T.astype(jnp.bfloat16).reshape(out_ref.shape[1:])
    for h in range(NH):
        out_ref[h] = result


def project_kernel(place_ref, g0, g1, g2, g3, w_hbm, mine_ref, other_ref, held, parts, acc, sems):
    y, z0 = place_ref[0], place_ref[1]
    copies = started(
        sems,
        [
            (w_hbm.at[i, k, pl.ds(lo, 2)], parts.at[i, k, pl.ds(lo, 2)])
            for i in range(NX)
            for k in range(NK)
            for lo in (0, 2)
        ],
    )
    for step, group in zip((0, 1, 3, 2), (g0, g1, g2, g3)):
        held[step] = group[...]
    for i in range(NX):
        step = (2 * y - i + NX) % NX
        heads = jnp.concatenate([held[step, j] for j in range(NH * NZ1)], axis=1)
        finished(copies[4 * i : 4 * i + 4])
        for k in range(NK):
            for b in range(2):
                columns = [parts[i, k, 2 * h + b].reshape(2 * HEAD, 256) for h in range(NH)]
                term = jnp.dot(
                    heads, jnp.concatenate(columns, axis=0), preferred_element_type=jnp.float32
                )
                lanes = slice(b * 256, b * 256 + 256)
                if i == 0:
                    acc[k, :, lanes] = term
                else:
                    acc[k, :, lanes] += term
    rows = mine_ref.shape[0]
    near_rows = pl.ds(pl.multiple_of(z0 * rows, rows), rows)
    far_rows = pl.ds(pl.multiple_of((1 - z0) * rows, rows), rows)
    for b in range(2):
        for k in range(NK):
            lo = (2 * b + k) * 256
            lanes = slice(b * 256, b * 256 + 256)
            mine_ref[:, lo : lo + 256] = acc[k, near_rows, lanes]
            other_ref[:, lo : lo + 256] = acc[k, far_rows, lanes].astype(jnp.bfloat16)


def per_device(hyena_feats, short_taps, decay_rate, residue, attn_qkv, out_weight):
    rows, width = hyena_feats.shape[1:]
    x, k, y = lax.axis_index("x"), lax.axis_index("k"), lax.axis_index("y")
    z1, z0 = lax.axis_index("z1"), lax.axis_index("z0")
    swap = [(0, 1), (1, 0)]
    short = jax.ShapeDtypeStruct
    bf16, f32 = jnp.bfloat16, jnp.float32
    dma = pltpu.SemaphoreType.DMA

    packed, tail = local_call(
        pack_kernel,
        (short((NZ, 3, rows, HEAD), bf16), short((3, 2, width), f32)),
        (SLOW, SLOW),
        "pack",
        10**8,
        (pltpu.VMEM((3, 16, width), bf16), dma((1 + NZ,))),
    )(attn_qkv, hyena_feats)
    qkv = lax.all_to_all(packed, ("z1", "z0"), 0, 0)
    halo = lax.ppermute(tail, ALL, moved(next_ctx))
    plane = short((rows, width), f32)
    poles = short(decay_rate.shape, f32)
    ends, prod, gate_rows = local_call(
        ends_kernel,
        (
            short((2, rows, HEAD), bf16),
            pltpu.HBM(plane.shape, f32),
            pltpu.HBM(plane.shape, f32),
        ),
        (SLOW, FAST, SLOW, SLOW),
        "ends",
        10**9,
        (
            pltpu.VMEM((3, rows, width), bf16),
            pltpu.VMEM(short_taps.shape, f32),
            pltpu.VMEM(poles.shape, f32),
            pltpu.VMEM(plane.shape, f32),
            pltpu.VMEM(plane.shape, f32),
            pltpu.VMEM((3, rows + 8, width), f32),
            dma((8,)),
            dma((2,)),
        ),
    )(hyena_feats, halo, short_taps, decay_rate)
    moved_weight = lax.ppermute(out_weight, ALL, moved(place_weight))
    spread = local_call(
        spread_kernel,
        short((NX, 2 * NZ + 2, rows, HEAD), bf16),
        (FAST, FAST),
        "spread",
        10**8,
        after=(moved_weight,),
    )(qkv, ends)
    far_own = lax.all_to_all(spread, "x", 0, 0)
    far_other = lax.ppermute(far_own, "k", swap)

    z = (2 * z1 + z0).reshape(1)
    half = short((NZ1, HEAD, out_weight.shape[1]), bf16)
    same, opposite = local_call(
        halves_kernel, (half, half), (SMEM, FAST), "halves", 10**8, after=(spread,)
    )(z, moved_weight)
    arrived = [same] + [
        lax.ppermute(opposite if steps % 2 else same, ALL, along_z(steps)) for steps in (1, 2, 3)
    ]
    placed = local_call(
        stack_kernel, short((NZ, *half.shape), bf16), (SMEM,) + (FAST,) * NZ, "stack", 10**8,
        after=(far_own,),
    )(z, *arrived)
    weight = lax.all_gather(placed, ("x", "k")).reshape(NX, NK, *placed.shape)

    where = jnp.stack([x, k])
    line = short((1, NZ * rows), f32)
    square = short((HEAD, NZ * rows), f32)
    partial = local_call(
        own_kernel, (line, line, square), (SMEM, FAST, FAST), "own", 2 * 10**9
    )(where, qkv, far_own)
    attended = local_call(
        other_kernel,
        short((NH, NZ1, NZ0 * rows, HEAD), bf16),
        (SMEM,) + (FAST,) * 5,
        "other",
        2 * 10**9,
        [pltpu.VMEM(part.shape, f32) for part in (line, line, square)],
    )(where, qkv, *partial, far_other)
    group = lax.all_to_all(attended.reshape(NH * NZ1, NZ0 * rows, HEAD), ("h", "z1"), 0, 0)
    groups = [group] + [
        lax.ppermute(group, "y", [(i, (i + step) % NY) for i in range(NY)]) for step in (1, 3, 2)
    ]

    parts = local_call(
        combine_kernel,
        short((NZ, *poles.shape), f32),
        (SMEM, SLOW, FAST, FAST),
        "combine",
        10**8,
        (pltpu.VMEM(poles.shape, f32), pltpu.VMEM((NX, NK, *poles.shape), f32), dma((1,))),
        after=(group,),
    )(jnp.stack([x, 2 * z1 + z0, k]), decay_rate, far_own, far_other)
    parts = lax.all_to_all(parts, ("z1", "z0"), 0, 0)

    mine, other = local_call(
        project_kernel,
        (short((rows, width), f32), short((rows, width), bf16)),
        (SMEM,) + (FAST,) * 4 + (SLOW,),
        "project",
        2 * 10**9,
        (
            pltpu.VMEM((NY, *group.shape), bf16),
            pltpu.VMEM(weight.shape, bf16),
            pltpu.VMEM((NK, NZ0 * rows, width // 2), f32),
            dma((4 * NX,)),
        ),
    )(jnp.stack([y, z0]), *groups, weight)
    received = lax.ppermute(other, "z0", swap)

    hyena_mixed = local_call(
        mix_kernel,
        short((rows, width), bf16),
        (SLOW, SLOW, FAST, SLOW, SLOW),
        "mix",
        4 * 10**9,
        (
            pltpu.VMEM(poles.shape, f32),
            pltpu.VMEM(poles.shape, f32),
            pltpu.VMEM(plane.shape, f32),
            pltpu.VMEM(plane.shape, f32),
            dma((4,)),
        ),
    )(decay_rate, residue, parts, prod, gate_rows)
    return hyena_mixed, (mine + received.astype(f32)).astype(bf16)


def solution(mesh):
    fine = Mesh(mesh.devices.reshape(NX, NZ1, NZ0, NK, NY, NH), ALL)
    ctx, tp = ("x", "z1", "z0", "k"), ("y", "h")
    return jax.shard_map(
        per_device,
        mesh=fine,
        in_specs=(
            P(None, ctx, tp),
            P(None, None, tp),
            P(None, tp),
            P(None, tp),
            P(None, ctx, tp),
            P(tp, ctx),
        ),
        out_specs=(P(ctx, tp), P(ctx, tp)),
        check_vma=False,
    )
```

```python
import math

import jax
import jax.numpy as jnp
from jax import lax
from jax.experimental import pallas as pl
from jax.experimental.pallas import tpu as pltpu
from jax.sharding import Mesh, PartitionSpec as P

HEAD = 128
NX, NZ1, NZ0, NK, NY, NH = 4, 2, 2, 2, 4, 2
NZ = NZ1 * NZ0
ALL = ("x", "z1", "z0", "k", "y", "h")
SIZES = dict(x=NX, z1=NZ1, z0=NZ0, k=NK, y=NY, h=NH)
SCALE = math.log2(math.e) / math.sqrt(HEAD)
VMEM = 48 * 1024 * 1024


def linear(**c):
    index = 0
    for name in ALL:
        index = index * SIZES[name] + c[name]
    return index


def places():
    for index in range(256):
        rest, c = index, {}
        for name in reversed(ALL):
            c[name] = rest % SIZES[name]
            rest //= SIZES[name]
        yield c


def moved(change):
    pairs = []
    for c in places():
        d = change(**c)
        if d is not None:
            pairs.append((linear(**c), linear(**dict(c, **d))))
    return pairs


def next_ctx(x, z1, z0, k, **_):
    place = ((x * NZ1 + z1) * NZ0 + z0) * NK + k + 1
    if place == NX * NZ * NK:
        return None
    return dict(x=place // (NZ * NK), z1=place // 4 % 2, z0=place // 2 % 2, k=place % 2)


def along_z(steps):
    def change(z1, z0, **_):
        z = (2 * z1 + z0 + steps) % NZ
        return dict(z1=z // 2, z0=z % 2)

    return moved(change)


def place_weight(x, z1, z0, k, y, h):
    return dict(x=(x + y) % NX, z1=h, z0=z0, k=k, y=x, h=z1)


SMEM = pl.BlockSpec(memory_space=pltpu.SMEM)
FAST = pl.BlockSpec(memory_space=pltpu.VMEM)
SLOW = pl.BlockSpec(memory_space=pltpu.HBM)
ANY = pl.BlockSpec(memory_space=pl.ANY)


def placed_out(out):
    return FAST if isinstance(out, jax.ShapeDtypeStruct) else SLOW


def local_call(kernel, out_shape, specs, name, flops, scratch=(), after=()):
    count = len(specs)

    def body(*refs):
        kernel(*refs[:count], *refs[count + len(after) :])

    call = pl.pallas_call(
        body,
        out_shape=out_shape,
        in_specs=list(specs) + [ANY] * len(after),
        out_specs=jax.tree.map(placed_out, out_shape),
        scratch_shapes=list(scratch),
        compiler_params=pltpu.CompilerParams(vmem_limit_bytes=VMEM),
        cost_estimate=pl.CostEstimate(flops=flops, bytes_accessed=2_000_000, transcendentals=0),
        name=name,
    )

    def placed(operand, spec):
        return pltpu.with_memory_space_constraint(operand, pltpu.HBM) if spec is SLOW else operand

    return lambda *operands: call(*map(placed, operands, specs), *after)


def gate(value, *after):
    return pl.pallas_call(
        lambda *refs: None,
        out_shape=jax.ShapeDtypeStruct(value.shape, value.dtype),
        in_specs=[ANY] * (1 + len(after)),
        out_specs=ANY,
        input_output_aliases={0: 0},
        name="gate",
    )(value, *after)


def started(sems, pairs):
    copies = [pltpu.make_async_copy(a, b, sems.at[i]) for i, (a, b) in enumerate(pairs)]
    for copy in copies:
        copy.start()
    return copies


def finished(copies):
    for copy in copies:
        copy.wait()


def fill_ext(x, halo_ref, ext, streams):
    for slot, stream in enumerate(streams):
        ext[slot, 6:8] = halo_ref[stream]
        for lo in range(0, x.shape[1], 32):
            ext[slot, lo + 8 : lo + 40] = x[slot, lo : lo + 32].astype(jnp.float32)


def featured_rows(ext, taps_ref, slot, stream, lo, rows):
    taps = taps_ref[stream]
    total = taps[0:1] * ext[slot, lo + 8 : lo + 8 + rows]
    for j in (1, 2):
        total += taps[j : j + 1] * ext[slot, lo + 8 - j : lo + 8 - j + rows]
    return total


def ends_kernel(
    feats, halo_ref, taps_hbm, decay_hbm, out_ref, prod_hbm, gate_hbm,
    x, taps, rate, prod, gate_rows, ext, sems, out_sems,
):
    rows, order = x.shape[1], rate.shape[0]
    half = rows // 2
    pieces = [(i, pl.ds(lo, half)) for i in range(3) for lo in (0, half)]
    pairs = [(taps_hbm, taps), (decay_hbm, rate)]
    pairs += [(feats.at[i, part, :], x.at[i, part, :]) for i, part in pieces]
    finished(started(sems, pairs))
    fill_ext(x, halo_ref, ext, (0, 1, 2))
    for lo in range(0, rows, 16):
        gate_rows[lo : lo + 16] = featured_rows(ext, taps, 0, 0, lo, 16)
        first = featured_rows(ext, taps, 1, 1, lo, 16)
        prod[lo : lo + 16] = first * featured_rows(ext, taps, 2, 2, lo, 16)
    written = started(out_sems, ((prod, prod_hbm), (gate_rows, gate_hbm)))
    decay = jnp.exp(-rate[...])

    def body(i, state):
        block = prod[pl.ds(pl.multiple_of(i * 8, 8), 8), :]
        for j in range(8):
            state = decay * state + block[j : j + 1]
        return state

    state = lax.fori_loop(0, rows // 8, body, jnp.zeros(rate.shape, jnp.float32))
    for j in range(state.shape[1] // HEAD):
        block = state[:, j * HEAD : (j + 1) * HEAD]
        high = block.astype(jnp.bfloat16)
        out_ref[0, j * order : (j + 1) * order] = high
        out_ref[1, j * order : (j + 1) * order] = (block - high.astype(jnp.float32)).astype(
            jnp.bfloat16
        )
    finished(written)


def combine_kernel(place_ref, rate_hbm, own_ref, other_ref, out_ref, rate_ref, ends, sems):
    finished(started(sems, ((rate_hbm, rate_ref),)))
    x, z, k = place_ref[0], place_ref[1], place_ref[2]
    rate = rate_ref[...]
    order = rate.shape[0]

    def over(blocks):
        return jnp.exp(rate * (-128.0 * jnp.maximum(blocks, 0).astype(jnp.float32)))

    for row in range(NX):
        for side, ref in enumerate((own_ref, other_ref)):
            both = ref[row, 2 * NZ].astype(jnp.float32) + ref[row, 2 * NZ + 1].astype(jnp.float32)
            for j in range(rate.shape[1] // HEAD):
                lanes = slice(j * HEAD, (j + 1) * HEAD)
                ends[row, side, :, lanes] = both[j * order : (j + 1) * order]

    def end_of(row, core):
        return ends[row, jnp.where(k == core, 0, 1)]

    step, across, rest = over(jnp.int32(1)), over(jnp.int32(NZ * NK)), over(NZ * NK - NK * z - NK)
    earlier = jnp.zeros(rate.shape, jnp.float32)
    for row in range(NX - 1):
        whole = rest * (step * end_of(row, 0) + end_of(row, 1))
        earlier = jnp.where(x > row, across * earlier + whole, earlier)
    for target in range(NZ):
        total = over(NK * target + k) * earlier
        for core in range(NK):
            blocks = (NK * target + k) - (NK * z + core) - 1
            total = total + jnp.where(blocks >= 0, over(blocks) * end_of(x, core), 0.0)
        out_ref[target] = total


def one_less_exp(y):
    series = 1.0 - y / 9.0
    for n in range(8, 1, -1):
        series = 1.0 - y / n * series
    return jnp.where(y < 0.5, y * series, 1.0 - jnp.exp(-y))


def mix_kernel(
    rate_hbm, residue_hbm, parts_ref, prod_hbm, gate_hbm, out_ref,
    rate, residue, prod, gate_rows, sems,
):
    pairs = ((rate_hbm, rate), (residue_hbm, residue), (prod_hbm, prod), (gate_hbm, gate_rows))
    finished(started(sems, pairs))
    rows, width = prod.shape
    decay = jnp.exp(-rate[...])
    start = parts_ref[0]
    for z in range(1, NZ):
        start = start + parts_ref[z]
    rho = residue[...] * jnp.sqrt(one_less_exp(2.0 * rate[...]) / rate.shape[0])
    sub = lax.broadcasted_iota(jnp.int32, (8, width), 0)

    def body(i, state):
        base = pl.multiple_of(i * 16, 16)
        mixed = []
        for half in range(2):
            block = prod[pl.ds(base + 8 * half, 8), :]
            conv = jnp.zeros((8, width), jnp.float32)
            for j in range(8):
                state = decay * state + block[j : j + 1]
                row = jnp.sum(rho * state, axis=0, keepdims=True)
                conv = jnp.where(sub == j, row, conv)
            mixed.append(conv * gate_rows[pl.ds(base + 8 * half, 8), :])
        out_ref[pl.ds(base, 16), :] = jnp.concatenate(mixed, axis=0).astype(jnp.bfloat16)
        return state

    lax.fori_loop(0, rows // 16, body, start)


def pack_kernel(qkv, feats, out_ref, halo_ref, tail, sems):
    rows = qkv.shape[1]
    lanes = [pl.ds(head * HEAD, HEAD) for head in range(NZ)]
    pairs = [(qkv.at[:, :, lanes[i]], out_ref.at[i]) for i in range(NZ)]
    pairs.append((feats.at[:, pl.ds(rows - 16, 16), :], tail))
    finished(started(sems, pairs))
    halo_ref[...] = tail[...].astype(jnp.float32)[:, 14:16]


def halves_kernel(place_ref, weight_ref, same_ref, other_ref):
    for half in range(NZ0):

        @pl.when(place_ref[0] % NZ0 == half)
        def _():
            for ref, z0 in ((same_ref, half), (other_ref, 1 - half)):
                for part in range(NZ1):
                    lo = (2 * part + z0) * HEAD
                    ref[part] = weight_ref[lo : lo + HEAD]


def stack_kernel(place_ref, *refs):
    for steps, ref in enumerate(refs[:-1]):
        refs[-1][(place_ref[0] + NZ - steps) % NZ] = ref[...]


def spread_kernel(qkv_ref, ends_ref, out_ref):
    for z in range(NZ):
        for i in range(out_ref.shape[0]):
            out_ref[i, 2 * z : 2 * z + 2] = qkv_ref[z, 1:]
    for i in range(out_ref.shape[0]):
        out_ref[i, 2 * NZ :] = ends_ref[...]


def folded(q, pairs, top, total, acc, visible=None):
    keys = pairs[:, 0].reshape(-1, HEAD)
    values = pairs[:, 1].reshape(-1, HEAD)
    s = lax.dot_general(keys, q, (((1,), (1,)), ((), ())), preferred_element_type=jnp.float32)
    if visible is not None:
        s = jnp.where(visible, s, -1e30)
    new = jnp.maximum(top, jnp.max(s, axis=0, keepdims=True))
    p = jnp.exp2((s - new) * SCALE)
    again = jnp.exp2((top - new) * SCALE)
    added = jnp.dot(values.T, p.astype(jnp.bfloat16), preferred_element_type=jnp.float32)
    return new, total * again + jnp.sum(p, axis=0, keepdims=True), acc * again + added


def pairs_of(ref, row):
    return ref[row, 0 : 2 * NZ].reshape(NZ, 2, HEAD, HEAD)


def fold_rows(x, q, ref, top, total, acc):
    for row in range(NX - 1):

        @pl.when(x > row)
        def _():
            top[...], total[...], acc[...] = folded(
                q, pairs_of(ref, row), top[...], total[...], acc[...]
            )


def own_kernel(place_ref, qkv_ref, kv_ref, top_ref, total_ref, acc_ref):
    x = place_ref[0]
    rows = NZ * HEAD
    q = qkv_ref[:, 0].reshape(rows, HEAD)
    col = lax.broadcasted_iota(jnp.int32, (1, rows), 1)
    row = lax.broadcasted_iota(jnp.int32, (rows, 1), 0)
    lowest = jnp.full((1, rows), -1e30, jnp.float32)
    nothing = jnp.zeros((1, rows), jnp.float32), jnp.zeros((HEAD, rows), jnp.float32)
    top_ref[...], total_ref[...], acc_ref[...] = folded(
        q, pairs_of(kv_ref, x), lowest, *nothing, row <= col
    )
    fold_rows(x, q, kv_ref, top_ref, total_ref, acc_ref)


def other_kernel(
    place_ref, qkv_ref, top_ref, total_ref, acc_ref, kv_ref, out_ref, top, total, acc
):
    x, k = place_ref[0], place_ref[1]
    rows = NZ * HEAD
    q = qkv_ref[:, 0].reshape(rows, HEAD)
    col = lax.broadcasted_iota(jnp.int32, (1, rows), 1)
    row = lax.broadcasted_iota(jnp.int32, (rows, 1), 0)
    here = (2 * (col // HEAD) + k) * HEAD + col % HEAD
    there = (2 * (row // HEAD) + 1 - k) * HEAD + row % HEAD
    top[...], total[...], acc[...] = folded(
        q, pairs_of(kv_ref, x), top_ref[...], total_ref[...], acc_ref[...], there <= here
    )
    fold_rows(x, q, kv_ref, top, total, acc)
    result = (acc[...] / total[...]).T.astype(jnp.bfloat16).reshape(out_ref.shape[1:])
    for h in range(NH):
        out_ref[h] = result


def project_kernel(place_ref, g0, g1, g2, g3, w_hbm, mine_ref, other_ref, held, parts, acc, sems):
    y, z0 = place_ref[0], place_ref[1]
    copies = started(
        sems,
        [
            (w_hbm.at[k, i, pl.ds(lo, 2)], parts.at[i, k, pl.ds(lo, 2)])
            for i in range(NX)
            for k in range(NK)
            for lo in (0, 2)
        ],
    )
    for step, group in zip((0, 1, 3, 2), (g0, g1, g2, g3)):
        held[step] = group[...]
    for i in range(NX):
        step = (2 * y - i + NX) % NX
        heads = jnp.concatenate([held[step, j] for j in range(NH * NZ1)], axis=1)
        finished(copies[4 * i : 4 * i + 4])
        for k in range(NK):
            for b in range(2):
                columns = [parts[i, k, 2 * h + b].reshape(2 * HEAD, 256) for h in range(NH)]
                term = jnp.dot(
                    heads, jnp.concatenate(columns, axis=0), preferred_element_type=jnp.float32
                )
                lanes = slice(b * 256, b * 256 + 256)
                if i == 0:
                    acc[k, :, lanes] = term
                else:
                    acc[k, :, lanes] += term
    rows = mine_ref.shape[0]
    near_rows = pl.ds(pl.multiple_of(z0 * rows, rows), rows)
    far_rows = pl.ds(pl.multiple_of((1 - z0) * rows, rows), rows)
    for b in range(2):
        for k in range(NK):
            lo = (2 * b + k) * 256
            lanes = slice(b * 256, b * 256 + 256)
            mine_ref[:, lo : lo + 256] = acc[k, near_rows, lanes]
            other_ref[:, lo : lo + 256] = acc[k, far_rows, lanes].astype(jnp.bfloat16)


def per_device(hyena_feats, short_taps, decay_rate, residue, attn_qkv, out_weight):
    rows, width = hyena_feats.shape[1:]
    x, k, y = lax.axis_index("x"), lax.axis_index("k"), lax.axis_index("y")
    z1, z0 = lax.axis_index("z1"), lax.axis_index("z0")
    swap = [(0, 1), (1, 0)]
    short = jax.ShapeDtypeStruct
    bf16, f32 = jnp.bfloat16, jnp.float32
    dma = pltpu.SemaphoreType.DMA

    packed, tail = local_call(
        pack_kernel,
        (short((NZ, 3, rows, HEAD), bf16), short((3, 2, width), f32)),
        (SLOW, SLOW),
        "pack",
        10**8,
        (pltpu.VMEM((3, 16, width), bf16), dma((1 + NZ,))),
    )(attn_qkv, hyena_feats)
    qkv = lax.all_to_all(packed, ("z1", "z0"), 0, 0)
    halo = lax.ppermute(tail, ALL, moved(next_ctx))
    plane = short((rows, width), f32)
    poles = short(decay_rate.shape, f32)
    ends, prod, gate_rows = local_call(
        ends_kernel,
        (
            short((2, rows, HEAD), bf16),
            pltpu.HBM(plane.shape, f32),
            pltpu.HBM(plane.shape, f32),
        ),
        (SLOW, FAST, SLOW, SLOW),
        "ends",
        10**9,
        (
            pltpu.VMEM((3, rows, width), bf16),
            pltpu.VMEM(short_taps.shape, f32),
            pltpu.VMEM(poles.shape, f32),
            pltpu.VMEM(plane.shape, f32),
            pltpu.VMEM(plane.shape, f32),
            pltpu.VMEM((3, rows + 8, width), f32),
            dma((8,)),
            dma((2,)),
        ),
    )(hyena_feats, halo, short_taps, decay_rate)
    moved_weight = lax.ppermute(out_weight, ALL, moved(place_weight))
    spread = local_call(
        spread_kernel,
        short((NX, 2 * NZ + 2, rows, HEAD), bf16),
        (FAST, FAST),
        "spread",
        10**8,
        after=(moved_weight,),
    )(qkv, ends)
    far_own = lax.all_to_all(spread, "x", 0, 0)
    far_other = lax.ppermute(far_own, "k", swap)

    z = (2 * z1 + z0).reshape(1)
    half = short((NZ1, HEAD, out_weight.shape[1]), bf16)
    same, opposite = local_call(
        halves_kernel, (half, half), (SMEM, FAST), "halves", 10**8, after=(spread,)
    )(z, moved_weight)
    arrived = [same] + [
        lax.ppermute(opposite if steps % 2 else same, ALL, along_z(steps)) for steps in (1, 2, 3)
    ]
    placed = local_call(
        stack_kernel, short((NZ, *half.shape), bf16), (SMEM,) + (FAST,) * NZ, "stack", 10**8,
        after=(far_own,),
    )(z, *arrived)
    weight = lax.all_gather(placed, ("k", "x")).reshape(NK, NX, *placed.shape)

    where = jnp.stack([x, k])
    line = short((1, NZ * rows), f32)
    square = short((HEAD, NZ * rows), f32)
    partial = local_call(
        own_kernel, (line, line, square), (SMEM, FAST, FAST), "own", 2 * 10**9
    )(where, qkv, far_own)
    attended = local_call(
        other_kernel,
        short((NH, NZ1, NZ0 * rows, HEAD), bf16),
        (SMEM,) + (FAST,) * 5,
        "other",
        2 * 10**9,
        [pltpu.VMEM(part.shape, f32) for part in (line, line, square)],
    )(where, qkv, *partial, far_other)
    group = lax.all_to_all(attended.reshape(NH * NZ1, NZ0 * rows, HEAD), ("h", "z1"), 0, 0)
    groups = [group] + [
        lax.ppermute(group, "y", [(i, (i + step) % NY) for i in range(NY)]) for step in (1, 3, 2)
    ]

    parts = local_call(
        combine_kernel,
        short((NZ, *poles.shape), f32),
        (SMEM, SLOW, FAST, FAST),
        "combine",
        10**8,
        (pltpu.VMEM(poles.shape, f32), pltpu.VMEM((NX, NK, *poles.shape), f32), dma((1,))),
        after=(group,),
    )(jnp.stack([x, 2 * z1 + z0, k]), decay_rate, far_own, far_other)
    parts = lax.all_to_all(parts, ("z1", "z0"), 0, 0)

    mine, other = local_call(
        project_kernel,
        (short((rows, width), f32), short((rows, width), bf16)),
        (SMEM,) + (FAST,) * 4 + (SLOW,),
        "project",
        2 * 10**9,
        (
            pltpu.VMEM((NY, *group.shape), bf16),
            pltpu.VMEM((NX, NK, *placed.shape), bf16),
            pltpu.VMEM((NK, NZ0 * rows, width // 2), f32),
            dma((4 * NX,)),
        ),
    )(jnp.stack([y, z0]), *groups, weight)
    received = lax.ppermute(other, "z0", swap)

    hyena_mixed = local_call(
        mix_kernel,
        short((rows, width), bf16),
        (SLOW, SLOW, FAST, SLOW, SLOW),
        "mix",
        4 * 10**9,
        (
            pltpu.VMEM(poles.shape, f32),
            pltpu.VMEM(poles.shape, f32),
            pltpu.VMEM(plane.shape, f32),
            pltpu.VMEM(plane.shape, f32),
            dma((4,)),
        ),
    )(decay_rate, residue, parts, prod, gate_rows)
    return hyena_mixed, (mine + received.astype(f32)).astype(bf16)


def solution(mesh):
    fine = Mesh(mesh.devices.reshape(NX, NZ1, NZ0, NK, NY, NH), ALL)
    ctx, tp = ("x", "z1", "z0", "k"), ("y", "h")
    return jax.shard_map(
        per_device,
        mesh=fine,
        in_specs=(
            P(None, ctx, tp),
            P(None, None, tp),
            P(None, tp),
            P(None, tp),
            P(None, ctx, tp),
            P(tp, ctx),
        ),
        out_specs=(P(ctx, tp), P(ctx, tp)),
        check_vma=False,
    )
```
